32 devices in a mesh: groups: 2 (over y), bins: 4 (over z), fdot: 4 (over x, core).
Axes of the slice: x: 2, y: 2, z: 4, core: 2. Of those that a mesh axis runs over, the one named last changes fastest.
Arguments:
- spectrum: float32 [2, 262144], P(None, ('groups', 'bins')), parts along dimension 1, may hold values from -80 to 80
- bank: bfloat16 [128, 2, 128], replicated, may hold values from -0.5 to 0.5
- fdot_index: int32 [32], P('fdot'), may hold values from 0 to 127
- harm_map: int32 [7, 4, 4], P(None, 'bins'), may hold values from 0 to 28672, as said below
Outputs:
- harmonic_power: float32 [32, 262144], P('fdot', ('groups', 'bins')), parts along dimension 1
The draws below stay inside these ranges and needn't reach their ends.
There are 2 independent parts, one for each index of `groups`. The reference program is written for one: setup_inputs(seed, part) draws one part's arguments, and reference() takes and returns one part's arrays. A program takes and returns all parts, laid end to end along the dimension named above; an argument that names none is the same for every part. Nothing has to cross between parts.
Inputs may be any that keep to these rules, and one draw needn't show every extreme that they name: harm_map[q, d] = (floor(d s / 8), s, (d * 32768 s / 8) mod 32768, p) with s = 4, 2, 6, 1, 3, 5, 7 for q = 0 .. 6 and a rounding phase p in 0 .. 7.
All inputs are finite; a program needn't handle non-finite values.
Results may differ from the reference program's by a relative error of at most 0.0003.
The reference program's roundings to bfloat16 on the way (of `normed` and `kernels`) count: a program that leaves them out, or rounds other values in their place, can miss the bound.
Values may be sent and summed in bfloat16 or wider, within the bound.
No kernel may reach another device: no remote copies, remote signals or barrier semaphores. Data moves between devices by JAX's collectives and lax.ppermute only.
A program may use at most 64 MiB of HBM per device.

```python
import math
import jax
import jax.numpy as jnp
from jax import lax

BLK = 32768
ZT = 32
W = 128
NBANK = 128
NFRAC = 7
BINS = 131072
NBLK = 4
N_BINS = 4


def draw_spectrum(key, part):
    key_scale = jax.random.fold_in(key, 11)
    key_base = jax.random.fold_in(key, 12)
    index = jnp.arange(BINS, dtype=jnp.float32)
    rough = jnp.exp(jax.random.uniform(key_scale, (BINS,), jnp.float32, math.log(0.3), math.log(3.0)))
    envelope = jnp.sqrt(1.0 + 2.0 * index / BINS)
    base = jnp.clip(jax.random.normal(key_base, (2, BINS), jnp.float32), -5.0, 5.0)
    target = base * (rough * envelope)[None, :]
    partner = jnp.concatenate([target[:, :1], target[:, :0:-1]], axis=1)
    even_real = 0.5 * (target[0] + partner[0])
    even_imag = 0.5 * (target[1] - partner[1])
    diff_real = 0.5 * (target[0] - partner[0])
    diff_imag = 0.5 * (target[1] + partner[1])
    angle = index * (math.pi / BINS)
    cosine = jnp.cos(angle)
    sine = jnp.sin(angle)
    odd_real = diff_real * cosine - diff_imag * sine
    odd_imag = diff_real * sine + diff_imag * cosine
    return jnp.stack([even_real - odd_imag, even_imag + odd_real]).astype(jnp.float32)


def draw_harm_map(key, part):
    numerators = jnp.array([4, 2, 6, 1, 3, 5, 7], jnp.int32)[:, None]
    blocks = jnp.arange(NBLK, dtype=jnp.int32)[None, :]
    source = jnp.broadcast_to(blocks * numerators // 8, (NFRAC, NBLK))
    stride = jnp.broadcast_to(numerators, (NFRAC, NBLK))
    offset = jnp.broadcast_to(blocks * numerators % 8 * (BLK // 8), (NFRAC, NBLK))
    phase = jax.random.randint(jax.random.fold_in(key, 21), (NFRAC, NBLK), 0, 8, dtype=jnp.int32)
    return jnp.stack([source, stride, offset, phase], axis=-1).astype(jnp.int32)


def with_ends(values, rng, least, high):
    extent = values.shape
    spot = [jax.random.randint(jax.random.fold_in(rng, axis), (), 0, extent[axis]) for axis in range(len(extent))]
    values = values.at[tuple(spot)].set(least)
    longest = extent.index(max(extent))
    spot[longest] = (spot[longest] + 1) % extent[longest]
    return values.at[tuple(spot)].set(high)


def scatter_about(own_key, shape, width, most, kind=jnp.bfloat16):
    drawn = jax.random.normal(own_key, shape, jnp.float32) * width
    return jnp.minimum(jnp.maximum(drawn, -most), most).astype(kind)


def setup_inputs(seed: int = 0, part: int = 0) -> dict:
    seeds = jax.random.split(jax.random.key(seed), 5)
    part_splits = jax.random.split(jax.random.fold_in(seeds[4], part), 5)
    spectrum = draw_spectrum(jax.random.fold_in(jax.random.fold_in(seeds[4], part), 71), part)
    bank = scatter_about(seeds[1], (NBANK, 2, W), W ** -0.5, 0.5)
    fdot_index = with_ends(jax.random.randint(seeds[2], (ZT,), 0, NBANK), jax.random.fold_in(seeds[2], 1), 0, NBANK - 1).astype(jnp.int32)
    harm_map = draw_harm_map(jax.random.fold_in(seeds[4], 71), part)
    return {"spectrum": spectrum, "bank": bank, "fdot_index": fdot_index, "harm_map": harm_map}


def unpack(packed, mirrored, positions, total_bins):
    real_a, imag_a = (packed[0], packed[1])
    real_b, imag_b = (mirrored[0], mirrored[1])
    even_real = 0.5 * (real_a + real_b)
    even_imag = 0.5 * (imag_a - imag_b)
    odd_real = 0.5 * (imag_a + imag_b)
    odd_imag = 0.5 * (real_b - real_a)
    angle = positions.astype(jnp.float32) * jnp.float32(math.pi / total_bins)
    cosine = jnp.cos(angle)
    sine = jnp.sin(angle)
    out_real = even_real + cosine * odd_real + sine * odd_imag
    out_imag = even_imag + cosine * odd_imag - sine * odd_real
    return (out_real, out_imag)

def toeplitz(kernel):
    row_count = kernel.shape[0]
    length = kernel.shape[1]
    padded = jnp.concatenate([kernel, jnp.zeros((row_count, length + 1), kernel.dtype)], axis=1)
    repeated = jnp.tile(padded, (1, length))[:, :2 * length * length]
    return repeated.reshape(row_count, length, 2 * length)

def template_weights(bank, fdot_index, kernel_len):
    n_bank = bank.shape[0]
    onehot = (fdot_index[:, None] == jnp.arange(n_bank, dtype=jnp.int32)[None, :]).astype(jnp.bfloat16)
    kernels = jnp.dot(onehot, bank.reshape(n_bank, 2 * kernel_len), preferred_element_type=jnp.float32).astype(jnp.bfloat16)
    real_part = toeplitz(kernels[:, :kernel_len])
    imag_part = toeplitz(kernels[:, kernel_len:])
    return jnp.stack([jnp.concatenate([real_part, -imag_part], axis=2), jnp.concatenate([imag_part, real_part], axis=2)])

def correlate(padded, weights, kernel_len):
    length = padded.shape[1] - kernel_len
    count = length // kernel_len
    lower = padded[:, :length].reshape(2, count, kernel_len)
    upper = padded[:, kernel_len:].reshape(2, count, kernel_len)
    stacked = jnp.concatenate([lower[0], upper[0], lower[1], upper[1]], axis=1)
    amps = jnp.einsum('ta,krca->krtc', stacked.astype(jnp.float32), weights.astype(jnp.float32))
    return (amps[0] * amps[0] + amps[1] * amps[1]).reshape(weights.shape[1], length)

def reference(spectrum, bank, fdot_index, harm_map):
    total_bins = BLK * N_BINS
    mirrored = jnp.concatenate([spectrum[:, :1], spectrum[:, :0:-1]], axis=1)
    positions = jnp.arange(total_bins, dtype=jnp.int32)
    out_real, out_imag = unpack(spectrum, mirrored, positions, total_bins)
    total_power = jnp.sum(out_real * out_real + out_imag * out_imag)
    scaling = lax.rsqrt(total_power / total_bins + 1e-06)
    normed = jnp.stack([out_real * scaling, out_imag * scaling]).astype(jnp.bfloat16)
    weights = template_weights(bank, fdot_index, W)
    half = W // 2
    padded = jnp.pad(normed, ((0, 0), (half, half)))

    def block_plane(start):
        window = lax.dynamic_slice(padded, (jnp.int32(0), start.astype(jnp.int32)), (2, BLK + W))
        return correlate(window, weights, W)
    planes = lax.map(block_plane, jnp.arange(N_BINS, dtype=jnp.int32) * BLK)
    plane = planes.transpose(1, 0, 2).reshape(ZT, total_bins)
    total = plane
    offsets = jnp.arange(BLK, dtype=jnp.int32)
    for fraction in range(NFRAC):
        entry = harm_map[fraction].astype(jnp.int32)
        source = entry[:, 0:1] * BLK + entry[:, 2:3] + (offsets[None, :] * entry[:, 1:2] + entry[:, 3:4]) // 8
        total = total + jnp.take(plane, source.reshape(-1), axis=1)
    return total * 0.125
```

```python
import functools
import math

import jax
import jax.numpy as jnp
from jax import lax
from jax.experimental import pallas as pl
from jax.experimental.pallas import tpu as pltpu
from jax.sharding import PartitionSpec as P

LANES = 128
STRIDE_TABLE = (4, 2, 6, 1, 3, 5, 7)
F32 = jnp.float32
BF16 = jnp.bfloat16


def from_partner(value, axis, mask):
    pairs = [(source, source ^ mask) for source in range(lax.axis_size(axis))]
    return lax.ppermute(value, axis, pairs)


def template_kernel(index_ref, bank_ref, out_ref):
    count = index_ref.shape[0]
    n_bank = bank_ref.shape[0]
    slots = lax.broadcasted_iota(jnp.int32, (count, n_bank), 1)
    onehot = (index_ref[...] == slots).astype(F32).astype(BF16)
    taps = jnp.dot(onehot, bank_ref[...], preferred_element_type=F32)
    zeros = jnp.zeros((1, LANES), F32)

    def banded(row):
        wide = jnp.broadcast_to(jnp.concatenate([row, zeros], axis=1), (LANES, 2 * LANES))
        return pltpu.roll(wide, 0, 1, stride=1, stride_axis=0)

    for t in range(count):
        real = banded(taps[t : t + 1, :LANES])
        imag = banded(taps[t : t + 1, LANES:])
        top, low = 2 * t * LANES, (2 * t + 1) * LANES
        out_ref[top : top + LANES, : 2 * LANES] = real.astype(BF16)
        out_ref[top : top + LANES, 2 * LANES :] = (-imag).astype(BF16)
        out_ref[low : low + LANES, : 2 * LANES] = imag.astype(BF16)
        out_ref[low : low + LANES, 2 * LANES :] = real.astype(BF16)


def template_rows(bank, fdot_index):
    count = fdot_index.shape[0]
    n_bank, _, taps = bank.shape
    rows = 2 * count * taps
    return pl.pallas_call(
        template_kernel,
        out_shape=jax.ShapeDtypeStruct((rows, 4 * taps), BF16),
        cost_estimate=pl.CostEstimate(
            flops=4 * rows * taps, bytes_accessed=8 * rows * taps, transcendentals=0
        ),
        name="template_rows",
    )(fdot_index.reshape(count, 1), bank.reshape(n_bank, 2 * taps))


def search_kernel(
    strides, sizes, meta_ref, twist_ref, base_ref, *refs
):
    block_rows, blocks, templates, moved = sizes
    own_ref, *rest = refs[: 1 + 2 * moved]
    rest = refs[1 : 1 + 2 * moved]
    weights_hbm, out_ref, raw, real, imag, weights, windows, acc, *more = refs[1 + 2 * moved :]
    planes = more[: len(strides)]
    copy_sem, weight_sem = more[len(strides) :]
    rows = block_rows * blocks
    total_bins = rows * LANES
    segments = block_rows // 8
    device = meta_ref[0]
    part = meta_ref[1]

    weight_copy = pltpu.make_async_copy(weights_hbm, weights, weight_sem)
    weight_copy.start()
    copies = []

    def fetch(source, start):
        size = source.shape[0]
        start = pl.multiple_of(start, size)
        copy = pltpu.make_async_copy(
            source, raw.at[pl.ds(start, size), :], copy_sem.at[len(copies)]
        )
        copy.start()
        copies.append(copy)

    fetch(own_ref, device * (2 * block_rows))
    for k in range(1, moved + 1):
        other = (device ^ k) * (2 * block_rows)
        fetch(rest[k - 1], other + part * block_rows)
        fetch(rest[moved + k - 1], other + (1 - part) * block_rows)
    for copy in copies:
        copy.wait()

    raw[2 * rows : 2 * rows + 16, :] = raw[0:16, :]
    row_ids = lax.broadcasted_iota(jnp.int32, (8, LANES), 0)
    lanes = lax.broadcasted_iota(jnp.int32, (8, LANES), 1)
    first_tile = raw[0:8, :]
    at_zero = (row_ids < 2) & (lanes == 0)
    zero_bin = jnp.sum(jnp.where(at_zero, first_tile, 0.0), keepdims=True)
    rest_tile = jnp.where(at_zero, 0.0, first_tile)

    def add_power(i, sums):
        out = []
        for j, value in enumerate(sums):
            tile = raw[pl.ds(pl.multiple_of((4 * i + j) * 8, 8), 8), :]
            out.append(value + tile * tile)
        return tuple(out)

    zero_tile = jnp.zeros((8, LANES), F32)
    sums = [rest_tile * rest_tile]
    for j in range(1, 4):
        tile = raw[8 * j : 8 * j + 8, :]
        sums.append(tile * tile)
    sums = lax.fori_loop(1, rows // 16, add_power, tuple(sums), unroll=7)
    power = jnp.sum((sums[0] + sums[1]) + (sums[2] + sums[3]), keepdims=True)
    mean = jnp.broadcast_to((power + zero_bin * zero_bin) * (1.0 / total_bins) + 1e-06, (8, LANES))
    scale = lax.rsqrt(mean)
    scale = scale * (1.5 - 0.5 * mean * scale * scale)
    half_scale = 0.5 * scale

    base_cos = base_ref[0:8, :]
    base_sin = base_ref[8:16, :]
    mirror_lane = (LANES - lanes) & (LANES - 1)
    mirror_row = 7 - row_ids
    real[0:8, :] = zero_tile
    imag[0:8, :] = zero_tile
    real[rows + 8 : rows + 16, :] = zero_tile
    imag[rows + 8 : rows + 16, :] = zero_tile

    def mirrored(start):
        near = raw[pl.ds(start + 2, 8, stride=2), :]
        far = raw[pl.ds(start, 8, stride=2), :]
        tile = jnp.where(lanes == 0, near, far)
        tile = jnp.take_along_axis(tile, mirror_lane, axis=1, mode="promise_in_bounds")
        return jnp.take_along_axis(tile, mirror_row, axis=0, mode="promise_in_bounds")

    def unpack(chunk, _):
        start = chunk * 16
        a0 = raw[pl.ds(start, 8, stride=2), :]
        a1 = raw[pl.ds(start + 1, 8, stride=2), :]
        back = 2 * rows - 16 - start
        b0 = mirrored(back)
        b1 = mirrored(back + 1)
        chunk_cos = twist_ref[0, chunk]
        chunk_sin = twist_ref[1, chunk]
        cosine = base_cos * chunk_cos - base_sin * chunk_sin
        sine = base_sin * chunk_cos + base_cos * chunk_sin
        odd_real = a1 + b1
        odd_imag = b0 - a0
        out_real = (a0 + b0) + cosine * odd_real + sine * odd_imag
        out_imag = (a1 - b1) + cosine * odd_imag - sine * odd_real
        place = pl.ds(pl.multiple_of(chunk * 8 + 8, 8), 8)
        real[place, :] = out_real * half_scale
        imag[place, :] = out_imag * half_scale
        return 0

    lax.fori_loop(0, rows // 8, unpack, 0, unroll=8)

    wide_lanes = lax.broadcasted_iota(jnp.int32, (segments, LANES), 1)
    for n, stride in enumerate(strides):
        first_row = meta_ref[2 + n] + 8
        for o in range(8):
            ahead = 2 * stride * 8 * o - LANES // 2
            skip, shift = ahead // LANES, ahead % LANES
            for c, source in enumerate((real, imag)):
                tiles = [
                    source[pl.ds(first_row + (skip + j), segments, stride=stride), :]
                    for j in range(3 if shift else 2)
                ]
                for half in range(2):
                    if shift:
                        tile = jnp.where(wide_lanes >= shift, tiles[half], tiles[half + 1])
                        tile = pltpu.roll(tile.astype(BF16), LANES - shift, 1)
                    else:
                        tile = tiles[half].astype(BF16)
                    at = (2 * c + half) * LANES
                    windows[n, o * segments : (o + 1) * segments, at : at + LANES] = tile

    weight_copy.wait()
    for n, stride in enumerate(strides):
        height = planes[n].shape[2]
        window = windows[n]
        for t in range(templates):
            top = 2 * t * LANES
            amps = [
                lax.dot_general(
                    weights[top + k * LANES : top + k * LANES + height, :],
                    window,
                    (((1,), (1,)), ((), ())),
                    preferred_element_type=F32,
                )
                for k in range(2)
            ]
            plane = amps[0] * amps[0] + amps[1] * amps[1]
            for h in range(2):
                planes[n][t, h] = plane[:, h * 4 * segments : (h + 1) * 4 * segments]

    for t in range(templates):
        for h in range(2):
            for b in range(8):
                total = None
                for n, stride in enumerate(strides):
                    plane = planes[n].at[t, h]
                    if stride == 8:
                        value = plane[pl.ds(b, LANES // 8, stride=8), :]
                    elif stride == 1:
                        late = meta_ref[2 + len(strides) + n] + b >= 8
                        value = jnp.where(late, plane[1 : 1 + LANES // 8, :], plane[: LANES // 8, :])
                    else:
                        first = (meta_ref[2 + len(strides) + n] + b * stride) >> 3
                        value = plane[pl.ds(first, LANES // 8, stride=stride), :]
                    total = value if total is None else total + value
                acc[pl.ds(b, LANES // 8, stride=8), :] = total * 0.125
            turned = acc[...].T
            for o in range(4):
                out_ref[pl.ds(templates * (4 * h + o) + t, segments, stride=8 * templates), :] = (
                    turned[o * segments : (o + 1) * segments, :]
                )


def body(spectrum, bank, fdot_index, harm_map):
    block_len = spectrum.shape[1]
    block_rows = block_len // LANES
    blocks = lax.axis_size("bins")
    templates = fdot_index.shape[0]
    rows = block_rows * blocks
    device = lax.axis_index("bins")
    part = lax.axis_index("fdot") % 2
    packed = spectrum.reshape(2, block_rows, LANES).transpose(1, 0, 2).reshape(2 * block_rows, LANES)
    mine = lax.dynamic_slice(packed, (part * block_rows, jnp.int32(0)), (block_rows, LANES))
    moved = [from_partner(mine, "bins", k) for k in range(1, blocks)]
    passed = [from_partner(value, "fdot", 1) for value in moved]
    weights = template_rows(bank, fdot_index)

    step = math.pi / (rows * LANES)
    fine = (jnp.arange(8 * LANES, dtype=F32) * F32(step)).reshape(8, LANES)
    base = jnp.concatenate([jnp.cos(fine), jnp.sin(fine)])
    coarse = jnp.arange(rows // 8, dtype=F32) * F32(step * 8 * LANES)
    twist = jnp.stack([jnp.cos(coarse), jnp.sin(coarse)])
    strides = STRIDE_TABLE + (8,)
    entries = harm_map[:, 0]
    starts = (entries[:, 0] * block_len + entries[:, 2]) // LANES
    meta = jnp.concatenate(
        [jnp.stack([device, part]), starts, (device * block_rows)[None], entries[:, 3]]
    ).astype(jnp.int32)

    segments = block_rows // 8
    heights = [min(LANES, 16 * stride + 16) for stride in strides]
    smem = pl.BlockSpec(memory_space=pltpu.SMEM)
    vmem = pl.BlockSpec(memory_space=pltpu.VMEM)
    hbm = pl.BlockSpec(memory_space=pl.ANY)
    out = pl.pallas_call(
        functools.partial(
            search_kernel, strides, (block_rows, blocks, templates, blocks - 1)
        ),
        out_shape=jax.ShapeDtypeStruct((block_rows * templates, LANES), F32),
        in_specs=[smem, smem, vmem] + [hbm] * (2 * blocks),
        out_specs=vmem,
        scratch_shapes=[
            pltpu.VMEM((2 * rows + 16, LANES), F32),
            pltpu.VMEM((rows + 16, LANES), F32),
            pltpu.VMEM((rows + 16, LANES), F32),
            pltpu.VMEM(weights.shape, BF16),
            pltpu.VMEM((len(strides), block_rows, 4 * LANES), BF16),
            pltpu.VMEM((LANES, 4 * segments), F32),
            *[pltpu.VMEM((templates, 2, height, block_rows // 2), F32) for height in heights],
            pltpu.SemaphoreType.DMA((2 * blocks - 1,)),
            pltpu.SemaphoreType.DMA,
        ],
        compiler_params=pltpu.CompilerParams(vmem_limit_bytes=56 * 2**20),
        name="search",
    )(meta, twist, base, packed, *moved, *passed, weights)
    return out.reshape(block_rows, templates, LANES).transpose(1, 0, 2).reshape(templates, block_len)


def solution(mesh):
    placed = (P(None, ("groups", "bins")), P(), P("fdot"), P(None, "bins", None))
    return jax.shard_map(
        body, mesh=mesh, in_specs=placed, out_specs=P("fdot", ("groups", "bins")), check_vma=False
    )
```

```python
import functools
import math

import jax
import jax.numpy as jnp
from jax import lax
from jax.experimental import pallas as pl
from jax.experimental.pallas import tpu as pltpu
from jax.sharding import PartitionSpec as P

LANES = 128
STRIDE_TABLE = (4, 2, 6, 1, 3, 5, 7)
F32 = jnp.float32
BF16 = jnp.bfloat16


def from_partner(value, axis, mask):
    pairs = [(source, source ^ mask) for source in range(lax.axis_size(axis))]
    return lax.ppermute(value, axis, pairs)


def template_kernel(step, index_ref, bank_ref, out_ref, base_ref, twist_ref):
    zeros = jnp.zeros((1, LANES), F32)

    def banded(row):
        wide = jnp.broadcast_to(jnp.concatenate([row, zeros], axis=1), (LANES, 2 * LANES))
        return pltpu.roll(wide, 0, 1, stride=1, stride_axis=0)

    for t in range(index_ref.shape[0]):
        taps = bank_ref[index_ref[t]].astype(F32)
        real = banded(taps[0:1])
        imag = banded(taps[1:2])
        top, low = 2 * t * LANES, (2 * t + 1) * LANES
        out_ref[top : top + LANES, : 2 * LANES] = real.astype(BF16)
        out_ref[top : top + LANES, 2 * LANES :] = (-imag).astype(BF16)
        out_ref[low : low + LANES, : 2 * LANES] = imag.astype(BF16)
        out_ref[low : low + LANES, 2 * LANES :] = real.astype(BF16)

    row_ids = lax.broadcasted_iota(jnp.int32, (8, LANES), 0)
    lanes = lax.broadcasted_iota(jnp.int32, (8, LANES), 1)
    fine = (row_ids * LANES + lanes).astype(F32) * F32(step)
    base_ref[0:8, :] = jnp.cos(fine)
    base_ref[8:16, :] = jnp.sin(fine)
    chunks = twist_ref.shape[1]
    coarse = lax.broadcasted_iota(jnp.int32, (chunks, LANES), 0).astype(F32)
    coarse = coarse * F32(step * 8 * LANES)
    twist_ref[0] = jnp.cos(coarse)
    twist_ref[1] = jnp.sin(coarse)


def template_rows(bank, fdot_index, rows):
    count = fdot_index.shape[0]
    taps = bank.shape[2]
    height = 2 * count * taps
    vmem = pl.BlockSpec(memory_space=pltpu.VMEM)
    return pl.pallas_call(
        functools.partial(template_kernel, math.pi / (rows * LANES)),
        in_specs=[pl.BlockSpec(memory_space=pltpu.SMEM), vmem],
        out_specs=[vmem, vmem, vmem],
        out_shape=[
            jax.ShapeDtypeStruct((height, 4 * taps), BF16),
            jax.ShapeDtypeStruct((16, LANES), F32),
            jax.ShapeDtypeStruct((2, rows // 8, LANES), F32),
        ],
        cost_estimate=pl.CostEstimate(
            flops=4 * height * taps, bytes_accessed=8 * height * taps, transcendentals=0
        ),
        compiler_params=pltpu.CompilerParams(vmem_limit_bytes=16 * 2**20),
        name="template_rows",
    )(fdot_index, bank)


def search_kernel(strides, sizes, meta_ref, map_ref, base_ref, twist_ref, *refs):
    block_rows, blocks, templates = sizes
    moved = blocks - 1
    own_ref = refs[0]
    rest = refs[1 : 1 + 2 * moved]
    weights_hbm, out_ref, raw, real, imag, weights, windows, acc, *more = refs[1 + 2 * moved :]
    planes = more[: len(strides)]
    copy_sem, weight_sem = more[len(strides) :]
    rows = block_rows * blocks
    total_bins = rows * LANES
    segments = block_rows // 8
    device = meta_ref[0]
    part = meta_ref[1]

    weight_copy = pltpu.make_async_copy(weights_hbm, weights, weight_sem)
    weight_copy.start()
    copies = []

    def fetch(source, start):
        size = source.shape[0]
        start = pl.multiple_of(start, size)
        copy = pltpu.make_async_copy(
            source, raw.at[pl.ds(start, size), :], copy_sem.at[len(copies)]
        )
        copy.start()
        copies.append(copy)

    fetch(own_ref, device * (2 * block_rows))
    for k in range(1, moved + 1):
        other = (device ^ k) * (2 * block_rows)
        fetch(rest[k - 1], other + part * block_rows)
        fetch(rest[moved + k - 1], other + (1 - part) * block_rows)
    for copy in copies:
        copy.wait()

    raw[2 * rows : 2 * rows + 16, :] = raw[0:16, :]
    row_ids = lax.broadcasted_iota(jnp.int32, (8, LANES), 0)
    lanes = lax.broadcasted_iota(jnp.int32, (8, LANES), 1)
    zero_tile = jnp.zeros((8, LANES), F32)
    half_scale = zero_tile + 0.001
    first_tile = raw[0:8, :]
    at_zero = (row_ids < 2) & (lanes == 0)
    zero_bin = jnp.sum(jnp.where(at_zero, first_tile, 0.0), keepdims=True)
    rest_tile = jnp.where(at_zero, 0.0, first_tile)

    def add_power(i, sums):
        out = []
        for j, value in enumerate(sums):
            tile = raw[pl.ds(pl.multiple_of((4 * i + j) * 8, 8), 8), :]
            out.append(value + tile * tile)
        return tuple(out)

    sums = [rest_tile * rest_tile]
    for j in range(1, 4):
        tile = raw[8 * j : 8 * j + 8, :]
        sums.append(tile * tile)
    sums = lax.fori_loop(1, rows // 16, add_power, tuple(sums), unroll=7)
    power = jnp.sum((sums[0] + sums[1]) + (sums[2] + sums[3]), keepdims=True)
    mean = jnp.broadcast_to((power + zero_bin * zero_bin) * (1.0 / total_bins) + 1e-06, (8, LANES))
    scale = lax.rsqrt(mean)
    scale = scale * (1.5 - 0.5 * mean * scale * scale)
    half_scale = 0.5 * scale

    base_cos = base_ref[0:8, :]
    base_sin = base_ref[8:16, :]
    mirror_lane = (LANES - lanes) & (LANES - 1)
    mirror_row = 7 - row_ids
    real[0:8, :] = zero_tile
    imag[0:8, :] = zero_tile
    real[rows + 8 : rows + 16, :] = zero_tile
    imag[rows + 8 : rows + 16, :] = zero_tile

    def mirrored(start):
        near = raw[pl.ds(start + 2, 8, stride=2), :]
        far = raw[pl.ds(start, 8, stride=2), :]
        tile = jnp.where(lanes == 0, near, far)
        tile = jnp.take_along_axis(tile, mirror_lane, axis=1, mode="promise_in_bounds")
        return jnp.take_along_axis(tile, mirror_row, axis=0, mode="promise_in_bounds")

    def unpack(chunk, _):
        start = chunk * 16
        a0 = raw[pl.ds(start, 8, stride=2), :]
        a1 = raw[pl.ds(start + 1, 8, stride=2), :]
        back = 2 * rows - 16 - start
        b0 = mirrored(back)
        b1 = mirrored(back + 1)
        chunk_cos = twist_ref[0, pl.ds(chunk, 1), :]
        chunk_sin = twist_ref[1, pl.ds(chunk, 1), :]
        cosine = base_cos * chunk_cos - base_sin * chunk_sin
        sine = base_sin * chunk_cos + base_cos * chunk_sin
        odd_real = a1 + b1
        odd_imag = b0 - a0
        out_real = (a0 + b0) + cosine * odd_real + sine * odd_imag
        out_imag = (a1 - b1) + cosine * odd_imag - sine * odd_real
        place = pl.ds(pl.multiple_of(chunk * 8 + 8, 8), 8)
        real[place, :] = out_real * half_scale
        imag[place, :] = out_imag * half_scale
        return 0

    lax.fori_loop(0, rows // 8, unpack, 0, unroll=8)

    wide_lanes = lax.broadcasted_iota(jnp.int32, (segments, LANES), 1)
    for n, stride in enumerate(strides):
        if stride == 8:
            first_row = device * block_rows + 8
        else:
            first_row = map_ref[n, 0] * block_rows + (map_ref[n, 2] >> 7) + 8
        for o in range(8):
            ahead = 2 * stride * 8 * o - LANES // 2
            skip, shift = ahead // LANES, ahead % LANES
            for c, source in enumerate((real, imag)):
                tiles = [
                    source[pl.ds(first_row + (skip + j), segments, stride=stride), :]
                    for j in range(3 if shift else 2)
                ]
                for half in range(2):
                    if shift:
                        tile = jnp.where(wide_lanes >= shift, tiles[half], tiles[half + 1])
                        tile = pltpu.roll(tile.astype(BF16), LANES - shift, 1)
                    else:
                        tile = tiles[half].astype(BF16)
                    at = (2 * c + half) * LANES
                    windows[n, o * segments : (o + 1) * segments, at : at + LANES] = tile

    weight_copy.wait()
    groups = 2
    share = templates // groups
    for g in range(groups):
        own = weights[2 * g * share * LANES : 2 * (g + 1) * share * LANES, :]
        own = own.reshape(2 * share, LANES, 4 * LANES)
        for n, stride in enumerate(strides):
            height = planes[n].shape[2]
            amps = lax.dot_general(
                own[:, :height].reshape(2 * share * height, 4 * LANES),
                windows[n],
                (((1,), (1,)), ((), ())),
                preferred_element_type=F32,
            ).reshape(share, 2, height, 2 * 4 * segments)
            for t in range(share):
                plane = amps[t, 0] * amps[t, 0] + amps[t, 1] * amps[t, 1]
                for h in range(2):
                    planes[n][g * share + t, h] = plane[:, h * 4 * segments : (h + 1) * 4 * segments]
    for t in range(templates):
        for h in range(2):
            for b in range(8):
                total = None
                for n, stride in enumerate(strides):
                    plane = planes[n].at[t, h]
                    if stride == 8:
                        value = plane[pl.ds(b, LANES // 8, stride=8), :]
                    elif stride == 1:
                        late = map_ref[n, 3] + b >= 8
                        value = jnp.where(late, plane[1 : 1 + LANES // 8, :], plane[: LANES // 8, :])
                    else:
                        first = (map_ref[n, 3] + b * stride) >> 3
                        value = plane[pl.ds(first, LANES // 8, stride=stride), :]
                    total = value if total is None else total + value
                acc[pl.ds(b, LANES // 8, stride=8), :] = total * 0.125
            turned = acc[...].T
            for o in range(4):
                out_ref[pl.ds(templates * (4 * h + o) + t, segments, stride=8 * templates), :] = (
                    turned[o * segments : (o + 1) * segments, :]
                )


def search(packed, moved, passed, weights, base, twist, harm_map, device, part, templates):
    blocks = 1 + len(moved)
    block_rows = packed.shape[0] // 2
    rows = block_rows * blocks
    strides = STRIDE_TABLE + (8,)
    segments = block_rows // 8
    heights = [min(LANES, 16 * stride + 16) for stride in strides]
    smem = pl.BlockSpec(memory_space=pltpu.SMEM)
    vmem = pl.BlockSpec(memory_space=pltpu.VMEM)
    hbm = pl.BlockSpec(memory_space=pl.ANY)
    scratch = [
        ((2 * rows + 16, LANES), F32),
        ((rows + 16, LANES), F32),
        ((rows + 16, LANES), F32),
        (weights.shape, BF16),
        ((len(strides), block_rows, 4 * LANES), BF16),
        ((LANES, 4 * segments), F32),
    ] + [((templates, 2, height, block_rows // 2), F32) for height in heights]
    used = sum(math.prod(shape) * jnp.dtype(kind).itemsize for shape, kind in scratch)
    return pl.pallas_call(
        functools.partial(search_kernel, strides, (block_rows, blocks, templates)),
        out_shape=jax.ShapeDtypeStruct((block_rows * templates, LANES), F32),
        in_specs=[smem, smem, vmem, vmem] + [hbm] * (2 * blocks),
        out_specs=vmem,
        scratch_shapes=[
            *[pltpu.VMEM(shape, kind) for shape, kind in scratch],
            pltpu.SemaphoreType.DMA((2 * blocks - 1,)),
            pltpu.SemaphoreType.DMA,
        ],
        compiler_params=pltpu.CompilerParams(vmem_limit_bytes=used + 12 * 2**20),
        name="search",
    )(
        jnp.stack([device, part]).astype(jnp.int32),
        harm_map.reshape(-1, 4),
        base,
        twist,
        packed,
        *moved,
        *passed,
        weights,
    )


def body(spectrum, bank, fdot_index, harm_map):
    block_len = spectrum.shape[1]
    block_rows = block_len // LANES
    blocks = lax.axis_size("bins")
    templates = fdot_index.shape[0]
    device = lax.axis_index("bins")
    part = lax.axis_index("fdot") & 1
    packed = spectrum.reshape(2, block_rows, LANES).transpose(1, 0, 2).reshape(2 * block_rows, LANES)
    mine = lax.dynamic_slice(packed, (part * block_rows, jnp.int32(0)), (block_rows, LANES))
    moved = [from_partner(mine, "bins", k) for k in range(1, blocks)]
    tables = template_rows(bank, fdot_index, block_rows * blocks)
    weights, base, twist = tables
    moved = [lax.optimization_barrier((value, base))[0] for value in moved]
    passed = [from_partner(value, "fdot", 1) for value in moved]
    out = search(packed, moved, passed, weights, base, twist, harm_map, device, part, templates)
    return out.reshape(block_rows, templates, LANES).transpose(1, 0, 2).reshape(templates, block_len)


def solution(mesh):
    placed = (P(None, ("groups", "bins")), P(), P("fdot"), P(None, "bins", None))
    return jax.shard_map(
        body, mesh=mesh, in_specs=placed, out_specs=P("fdot", ("groups", "bins")), check_vma=False
    )
```

```python
import functools
import math

import jax
import jax.numpy as jnp
from jax import lax
from jax.experimental import pallas as pl
from jax.experimental.pallas import tpu as pltpu
from jax.sharding import PartitionSpec as P

LANES = 128
STRIDE_TABLE = (4, 2, 6, 1, 3, 5, 7)
F32 = jnp.float32
BF16 = jnp.bfloat16


def from_partner(value, axis, mask):
    pairs = [(source, source ^ mask) for source in range(lax.axis_size(axis))]
    return lax.ppermute(value, axis, pairs)


def template_kernel(
    step, packed_hbm, index_hbm, bank_hbm, own_ref, out_ref, base_ref, twist_ref, index_ref, bank_ref, sem
):
    pairs = ((index_hbm, index_ref), (bank_hbm, bank_ref), (packed_hbm, own_ref))
    copies = [pltpu.make_async_copy(source, to, sem.at[i]) for i, (source, to) in enumerate(pairs)]
    for copy in copies:
        copy.start()

    row_ids = lax.broadcasted_iota(jnp.int32, (8, LANES), 0)
    lanes = lax.broadcasted_iota(jnp.int32, (8, LANES), 1)
    fine = (row_ids * LANES + lanes).astype(F32) * F32(step)
    base_ref[0:8, :] = jnp.cos(fine)
    base_ref[8:16, :] = jnp.sin(fine)
    chunks = twist_ref.shape[1]
    coarse = lax.broadcasted_iota(jnp.int32, (chunks, LANES), 0).astype(F32)
    coarse = coarse * F32(step * 8 * LANES)
    twist_ref[0] = jnp.cos(coarse)
    twist_ref[1] = jnp.sin(coarse)

    copies[0].wait()
    copies[1].wait()
    zeros = jnp.zeros((1, LANES), F32)

    def banded(row):
        wide = jnp.broadcast_to(jnp.concatenate([row, zeros], axis=1), (LANES, 2 * LANES))
        return pltpu.roll(wide, 0, 1, stride=1, stride_axis=0)

    for t in range(index_ref.shape[0]):
        taps = bank_ref[index_ref[t]].astype(F32)
        real = banded(taps[0:1])
        imag = banded(taps[1:2])
        top, low = 2 * t * LANES, (2 * t + 1) * LANES
        out_ref[top : top + LANES, : 2 * LANES] = real.astype(BF16)
        out_ref[top : top + LANES, 2 * LANES :] = (-imag).astype(BF16)
        out_ref[low : low + LANES, : 2 * LANES] = imag.astype(BF16)
        out_ref[low : low + LANES, 2 * LANES :] = real.astype(BF16)
    copies[2].wait()


def template_rows(packed, bank, fdot_index, rows):
    count = fdot_index.shape[0]
    taps = bank.shape[2]
    height = 2 * count * taps
    vmem = pl.BlockSpec(memory_space=pltpu.VMEM)
    return pl.pallas_call(
        functools.partial(template_kernel, math.pi / (rows * LANES)),
        in_specs=[pl.BlockSpec(memory_space=pltpu.HBM)] * 3,
        out_specs=[vmem] * 4,
        out_shape=[
            jax.ShapeDtypeStruct(packed.shape, F32),
            jax.ShapeDtypeStruct((height, 4 * taps), BF16),
            jax.ShapeDtypeStruct((16, LANES), F32),
            jax.ShapeDtypeStruct((2, rows // 8, LANES), F32),
        ],
        scratch_shapes=[
            pltpu.SMEM(fdot_index.shape, jnp.int32),
            pltpu.VMEM(bank.shape, BF16),
            pltpu.SemaphoreType.DMA((3,)),
        ],
        cost_estimate=pl.CostEstimate(
            flops=4 * height * taps, bytes_accessed=8 * height * taps, transcendentals=0
        ),
        compiler_params=pltpu.CompilerParams(vmem_limit_bytes=16 * 2**20),
        name="template_rows",
    )(packed, fdot_index, bank)


def search_kernel(strides, sizes, meta_ref, map_ref, base_ref, twist_ref, *refs):
    block_rows, blocks, templates = sizes
    moved = blocks - 1
    own_ref = refs[0]
    rest = refs[1 : 1 + 2 * moved]
    weights, out_ref, raw, real, imag, acc, flat, *more = refs[1 + 2 * moved :]
    windows = more[: len(strides)]
    more = more[len(strides) :]
    groups = 2
    share = templates // groups
    planes = [more[g * len(strides) : (g + 1) * len(strides)] for g in range(groups)]
    copy_sem = more[groups * len(strides)]
    rows = block_rows * blocks
    total_bins = rows * LANES
    segments = block_rows // 8
    device = meta_ref[0]
    part = meta_ref[1]
    column = meta_ref[2]

    copies = []

    def fetch(source, start):
        size = source.shape[0]
        start = pl.multiple_of(start, size)
        copy = pltpu.make_async_copy(
            source, raw.at[pl.ds(start, size), :], copy_sem.at[len(copies)]
        )
        copy.start()
        copies.append(copy)

    fetch(own_ref, device * (2 * block_rows))
    masks = [1]
    for pair in range(2, blocks, 2):
        masks += [pair + 1 - column, pair + column]
    for k, mask in enumerate(masks):
        other = (device ^ mask) * (2 * block_rows)
        fetch(rest[k], other + part * block_rows)
        fetch(rest[moved + k], other + (1 - part) * block_rows)
    halves = [own_ref.at[:block_rows], own_ref.at[block_rows:], *rest]
    sums = [jnp.zeros((8, LANES), F32)] * 4
    for half in halves:
        for i in range(1, block_rows // 8):
            tile = half[8 * i : 8 * i + 8, :]
            sums[i % 4] = sums[i % 4] + tile * tile
    for copy in copies:
        copy.wait()
    raw[2 * rows : 2 * rows + 16, :] = raw[0:16, :]
    row_ids = lax.broadcasted_iota(jnp.int32, (8, LANES), 0)
    lanes = lax.broadcasted_iota(jnp.int32, (8, LANES), 1)
    zero_tile = jnp.zeros((8, LANES), F32)
    half_scale = zero_tile + 0.001
    first_tile = raw[0:8, :]
    at_zero = (row_ids < 2) & (lanes == 0)
    zero_bin = jnp.sum(jnp.where(at_zero, first_tile, 0.0), keepdims=True)
    first_tile = jnp.where(at_zero, 0.0, first_tile)
    sums[0] = sums[0] + first_tile * first_tile
    for j in range(1, 2 * blocks):
        tile = raw[j * block_rows : j * block_rows + 8, :]
        sums[j % 4] = sums[j % 4] + tile * tile
    power = jnp.sum((sums[0] + sums[1]) + (sums[2] + sums[3]), keepdims=True)
    mean = jnp.broadcast_to((power + zero_bin * zero_bin) * (1.0 / total_bins) + 1e-06, (8, LANES))
    scale = lax.rsqrt(mean)
    scale = scale * (1.5 - 0.5 * mean * scale * scale)
    half_scale = 0.5 * scale

    base_cos = base_ref[0:8, :]
    base_sin = base_ref[8:16, :]
    mirror_lane = (LANES - lanes) & (LANES - 1)
    mirror_row = 7 - row_ids
    real[0:8, :] = zero_tile
    imag[0:8, :] = zero_tile
    real[rows + 8 : rows + 16, :] = zero_tile
    imag[rows + 8 : rows + 16, :] = zero_tile

    def mirrored(start):
        near = raw[pl.ds(start + 2, 8, stride=2), :]
        far = raw[pl.ds(start, 8, stride=2), :]
        tile = jnp.where(lanes == 0, near, far)
        tile = jnp.take_along_axis(tile, mirror_lane, axis=1, mode="promise_in_bounds")
        return jnp.take_along_axis(tile, mirror_row, axis=0, mode="promise_in_bounds")

    def unpack(chunk, _):
        start = chunk * 16
        a0 = raw[pl.ds(start, 8, stride=2), :]
        a1 = raw[pl.ds(start + 1, 8, stride=2), :]
        back = 2 * rows - 16 - start
        b0 = mirrored(back)
        b1 = mirrored(back + 1)
        chunk_cos = twist_ref[0, pl.ds(chunk, 1), :]
        chunk_sin = twist_ref[1, pl.ds(chunk, 1), :]
        cosine = base_cos * chunk_cos - base_sin * chunk_sin
        sine = base_sin * chunk_cos + base_cos * chunk_sin
        odd_real = a1 + b1
        odd_imag = b0 - a0
        out_real = (a0 + b0) + cosine * odd_real + sine * odd_imag
        out_imag = (a1 - b1) + cosine * odd_imag - sine * odd_real
        place = pl.ds(pl.multiple_of(chunk * 8 + 8, 8), 8)
        real[place, :] = out_real * half_scale
        imag[place, :] = out_imag * half_scale
        return 0

    group = 16
    lowest = jnp.maximum(device * (block_rows // 8) - 1, 0) // (8 * group)
    highest = jnp.minimum(((device + 1) * block_rows + 8 * group) // (8 * group), rows // (8 * group))

    def unpack_group(i, _):
        for j in range(group):
            unpack(i * group + j, 0)
        return 0

    lax.fori_loop(lowest, highest, unpack_group, 0)

    wide_lanes = lax.broadcasted_iota(jnp.int32, (segments, LANES), 1)
    def make_windows(n, stride):
        if stride == 8:
            first_row = device * block_rows + 8
        else:
            first_row = map_ref[n, 0] * block_rows + (map_ref[n, 2] >> 7) + 8
        for o in range(8):
            ahead = 2 * stride * 8 * o - LANES // 2
            skip, shift = ahead // LANES, ahead % LANES
            for c, source in enumerate((real, imag)):
                tiles = [
                    source[pl.ds(first_row + (skip + j), segments, stride=stride), :]
                    for j in range(3 if shift else 2)
                ]
                for half in range(2):
                    if shift:
                        tile = jnp.where(wide_lanes >= shift, tiles[half], tiles[half + 1])
                        tile = pltpu.roll(tile.astype(BF16), LANES - shift, 1)
                    else:
                        tile = tiles[half].astype(BF16)
                    at = (2 * c + half) * LANES
                    windows[n][o * segments : (o + 1) * segments, at : at + LANES] = tile

    def add_up(first, last):
        for t in range(first, last):
            for h in range(2):
                shared = {
                    n: [planes[t // share][n][t % share, h, pl.ds(c, LANES // 8, stride=stride), :] for c in range(stride + 1)]
                    for n, stride in enumerate(strides)
                    if stride <= 2
                }
                for b in range(8):
                    total = None
                    for n, stride in enumerate(strides):
                        plane = planes[t // share][n].at[t % share, h]
                        if stride == 8:
                            value = plane[pl.ds(b, LANES // 8, stride=8), :]
                        elif stride <= 2:
                            first = (map_ref[n, 3] + b * stride) >> 3
                            value = shared[n][0]
                            for c in range(1, stride + 1):
                                value = jnp.where(first == c, shared[n][c], value)
                        else:
                            first = (map_ref[n, 3] + b * stride) >> 3
                            value = plane[pl.ds(first, LANES // 8, stride=stride), :]
                        total = value if total is None else total + value
                    acc[(2 * t + h) % 2, pl.ds(b, LANES // 8, stride=8), :] = total * 0.125
                turned = acc[(2 * t + h) % 2].T
                for o in range(4):
                    flat[t % 2, pl.ds(4 * h + o, segments, stride=8), :] = turned[o * segments : (o + 1) * segments, :]
            for m in range(segments):
                out_ref[pl.ds(8 * templates * m + t, 8, stride=templates), :] = flat[t % 2, 8 * m : 8 * m + 8, :]

    for g in range(groups):
        own = weights[2 * g * share * LANES : 2 * (g + 1) * share * LANES, :]
        own = own.reshape(2 * share, LANES, 4 * LANES)
        for n, stride in enumerate(strides):
            height = planes[g][n].shape[2]
            if g == 0:
                make_windows(n, stride)
            amps = lax.dot_general(
                own[:, :height].reshape(2 * share * height, 4 * LANES),
                windows[n][...],
                (((1,), (1,)), ((), ())),
                preferred_element_type=F32,
            ).reshape(share, 2, height, 2 * 4 * segments)
            for t in range(share):
                plane = amps[t, 0] * amps[t, 0] + amps[t, 1] * amps[t, 1]
                for h in range(2):
                    planes[g][n][t, h] = plane[:, h * 4 * segments : (h + 1) * 4 * segments]
        if g:
            add_up((g - 1) * share, g * share)
    add_up((groups - 1) * share, templates)


def search(packed, moved, passed, weights, base, twist, harm_map, place, templates):
    blocks = 1 + len(moved)
    block_rows = packed.shape[0] // 2
    rows = block_rows * blocks
    strides = STRIDE_TABLE + (8,)
    segments = block_rows // 8
    heights = [min(LANES, 16 * stride + 16) for stride in strides]
    smem = pl.BlockSpec(memory_space=pltpu.SMEM)
    vmem = pl.BlockSpec(memory_space=pltpu.VMEM)
    scratch = [
        ((2 * rows + 16, LANES), F32),
        ((rows + 16, LANES), F32),
        ((rows + 16, LANES), F32),
        ((2, LANES, 4 * segments), F32),
        ((2, block_rows, LANES), F32),
    ] + len(strides) * [((block_rows, 4 * LANES), BF16)] + 2 * [((templates // 2, 2, height, block_rows // 2), F32) for height in heights]
    used = sum(math.prod(shape) * jnp.dtype(kind).itemsize for shape, kind in scratch)
    return pl.pallas_call(
        functools.partial(search_kernel, strides, (block_rows, blocks, templates)),
        out_shape=jax.ShapeDtypeStruct((block_rows * templates, LANES), F32),
        in_specs=[smem, smem] + [vmem] * (2 + 2 * blocks),
        out_specs=vmem,
        scratch_shapes=[
            *[pltpu.VMEM(shape, kind) for shape, kind in scratch],
            pltpu.SemaphoreType.DMA((2 * blocks - 1,)),
        ],
        compiler_params=pltpu.CompilerParams(vmem_limit_bytes=used + 12 * 2**20),
        name="search",
    )(
        place,
        harm_map,
        base,
        twist,
        packed,
        *moved,
        *passed,
        weights,
    )


def from_across(value, pair):
    blocks, peers = lax.axis_size("bins"), lax.axis_size("fdot")
    pairs = [
        (peers * d + f, peers * (d ^ (pair + 1 - (f >> 1) % 2)) + f)
        for d in range(blocks)
        for f in range(peers)
    ]
    return lax.ppermute(value, ("bins", "fdot"), pairs)


def body(spectrum, bank, fdot_index, harm_map):
    block_len = spectrum.shape[1]
    block_rows = block_len // LANES
    blocks = lax.axis_size("bins")
    templates = fdot_index.shape[0]
    device = lax.axis_index("bins")
    peer = lax.axis_index("fdot")
    part = peer & 1
    place = jnp.stack([device, part, (peer >> 1) & 1]).astype(jnp.int32)
    packed = spectrum.reshape(2, block_rows, LANES).transpose(1, 0, 2).reshape(2 * block_rows, LANES)
    mine = lax.dynamic_slice(packed, (part * block_rows, jnp.int32(0)), (block_rows, LANES))
    across = [from_across(mine, pair) for pair in range(2, blocks, 2)]
    steps = harm_map.reshape(-1, 4)
    fdot_index, steps, place = lax.optimization_barrier((fdot_index, steps, place))
    own, weights, base, twist = template_rows(packed, bank, fdot_index, block_rows * blocks)
    mine, base = lax.optimization_barrier((mine, base))
    moved = [from_partner(mine, "bins", 1)]
    for value in across:
        value = lax.optimization_barrier((value, base))[0]
        moved += [value, from_partner(value, "fdot", 2)]
    passed = [from_partner(value, "fdot", 1) for value in moved]
    out = search(own, moved, passed, weights, base, twist, steps, place, templates)
    return out.reshape(block_rows, templates, LANES).transpose(1, 0, 2).reshape(templates, block_len)


def solution(mesh):
    placed = (P(None, ("groups", "bins")), P(), P("fdot"), P(None, "bins", None))
    return jax.shard_map(
        body, mesh=mesh, in_specs=placed, out_specs=P("fdot", ("groups", "bins")), check_vma=False
    )
```

```python
import functools
import math

import jax
import jax.numpy as jnp
from jax import lax
from jax.experimental import pallas as pl
from jax.experimental.pallas import tpu as pltpu
from jax.sharding import PartitionSpec as P

LANES = 128
STRIDE_TABLE = (4, 2, 6, 1, 3, 5, 7)
F32 = jnp.float32
BF16 = jnp.bfloat16


def from_partner(value, axis, mask):
    pairs = [(source, source ^ mask) for source in range(lax.axis_size(axis))]
    return lax.ppermute(value, axis, pairs)


def template_kernel(
    step, index_hbm, bank_hbm, out_ref, base_ref, twist_ref, index_ref, bank_ref, sem
):
    pairs = ((index_hbm, index_ref), (bank_hbm, bank_ref))
    copies = [pltpu.make_async_copy(source, to, sem.at[i]) for i, (source, to) in enumerate(pairs)]
    for copy in copies:
        copy.start()

    row_ids = lax.broadcasted_iota(jnp.int32, (8, LANES), 0)
    lanes = lax.broadcasted_iota(jnp.int32, (8, LANES), 1)
    fine = (row_ids * LANES + lanes).astype(F32) * F32(step)
    base_ref[0:8, :] = jnp.cos(fine)
    base_ref[8:16, :] = jnp.sin(fine)
    chunks = twist_ref.shape[1]
    coarse = lax.broadcasted_iota(jnp.int32, (chunks, LANES), 0).astype(F32)
    coarse = coarse * F32(step * 8 * LANES)
    twist_ref[0] = jnp.cos(coarse)
    twist_ref[1] = jnp.sin(coarse)

    copies[0].wait()
    copies[1].wait()
    zeros = jnp.zeros((1, LANES), F32)

    def banded(row):
        wide = jnp.broadcast_to(jnp.concatenate([row, zeros], axis=1), (LANES, 2 * LANES))
        return pltpu.roll(wide, 0, 1, stride=1, stride_axis=0)

    for t in range(index_ref.shape[0]):
        taps = bank_ref[index_ref[t]].astype(F32)
        real = banded(taps[0:1])
        imag = banded(taps[1:2])
        top, low = 2 * t * LANES, (2 * t + 1) * LANES
        out_ref[top : top + LANES, : 2 * LANES] = real.astype(BF16)
        out_ref[top : top + LANES, 2 * LANES :] = (-imag).astype(BF16)
        out_ref[low : low + LANES, : 2 * LANES] = imag.astype(BF16)
        out_ref[low : low + LANES, 2 * LANES :] = real.astype(BF16)


def template_rows(bank, fdot_index, rows):
    count = fdot_index.shape[0]
    taps = bank.shape[2]
    height = 2 * count * taps
    vmem = pl.BlockSpec(memory_space=pltpu.VMEM)
    return pl.pallas_call(
        functools.partial(template_kernel, math.pi / (rows * LANES)),
        in_specs=[pl.BlockSpec(memory_space=pltpu.HBM)] * 2,
        out_specs=[vmem] * 3,
        out_shape=[
            jax.ShapeDtypeStruct((height, 4 * taps), BF16),
            jax.ShapeDtypeStruct((16, LANES), F32),
            jax.ShapeDtypeStruct((2, rows // 8, LANES), F32),
        ],
        scratch_shapes=[
            pltpu.SMEM(fdot_index.shape, jnp.int32),
            pltpu.VMEM(bank.shape, BF16),
            pltpu.SemaphoreType.DMA((2,)),
        ],
        cost_estimate=pl.CostEstimate(
            flops=4 * height * taps, bytes_accessed=8 * height * taps, transcendentals=0
        ),
        compiler_params=pltpu.CompilerParams(vmem_limit_bytes=16 * 2**20),
        name="template_rows",
    )(fdot_index, bank)


def search_kernel(strides, sizes, meta_ref, map_ref, base_ref, twist_ref, *refs):
    block_rows, blocks, templates, layout = sizes
    pieces = refs[: 2 * len(layout)]
    weights, out_ref, raw, real, imag, acc, flat, *more = refs[2 * len(layout) :]
    windows = more[: len(strides)]
    more = more[len(strides) :]
    groups = 2
    share = templates // groups
    planes = [more[g * len(strides) : (g + 1) * len(strides)] for g in range(groups)]
    rows = block_rows * blocks
    total_bins = rows * LANES
    segments = block_rows // 8
    device = meta_ref[0]
    part = meta_ref[1]
    column = meta_ref[2]

    sums = [jnp.zeros((8, LANES), F32)] * 4
    for i, source in enumerate(pieces):
        pair, cross = layout[i % len(layout)]
        mask = pair + (1 - column if cross else column) if pair > 1 else pair
        half = part if i < len(layout) else 1 - part
        start = pl.multiple_of((device ^ mask) * (2 * block_rows) + half * block_rows, block_rows)
        for j in range(block_rows // 8):
            tile = source[8 * j : 8 * j + 8, :]
            raw[pl.ds(start + 8 * j, 8), :] = tile
            if j:
                sums[j % 4] = sums[j % 4] + tile * tile
    raw[2 * rows : 2 * rows + 16, :] = raw[0:16, :]
    row_ids = lax.broadcasted_iota(jnp.int32, (8, LANES), 0)
    lanes = lax.broadcasted_iota(jnp.int32, (8, LANES), 1)
    zero_tile = jnp.zeros((8, LANES), F32)
    half_scale = zero_tile + 0.001
    first_tile = raw[0:8, :]
    at_zero = (row_ids < 2) & (lanes == 0)
    zero_bin = jnp.sum(jnp.where(at_zero, first_tile, 0.0), keepdims=True)
    first_tile = jnp.where(at_zero, 0.0, first_tile)
    sums[0] = sums[0] + first_tile * first_tile
    for j in range(1, 2 * blocks):
        tile = raw[j * block_rows : j * block_rows + 8, :]
        sums[j % 4] = sums[j % 4] + tile * tile
    power = jnp.sum((sums[0] + sums[1]) + (sums[2] + sums[3]), keepdims=True)
    mean = jnp.broadcast_to((power + zero_bin * zero_bin) * (1.0 / total_bins) + 1e-06, (8, LANES))
    scale = lax.rsqrt(mean)
    scale = scale * (1.5 - 0.5 * mean * scale * scale)
    half_scale = 0.5 * scale

    base_cos = base_ref[0:8, :]
    base_sin = base_ref[8:16, :]
    mirror_lane = (LANES - lanes) & (LANES - 1)
    mirror_row = 7 - row_ids
    real[0:8, :] = zero_tile
    imag[0:8, :] = zero_tile
    real[rows + 8 : rows + 16, :] = zero_tile
    imag[rows + 8 : rows + 16, :] = zero_tile

    def mirrored(start):
        near = raw[pl.ds(start + 2, 8, stride=2), :]
        far = raw[pl.ds(start, 8, stride=2), :]
        tile = jnp.where(lanes == 0, near, far)
        tile = jnp.take_along_axis(tile, mirror_lane, axis=1, mode="promise_in_bounds")
        return jnp.take_along_axis(tile, mirror_row, axis=0, mode="promise_in_bounds")

    def unpack(chunk, _):
        start = chunk * 16
        a0 = raw[pl.ds(start, 8, stride=2), :]
        a1 = raw[pl.ds(start + 1, 8, stride=2), :]
        back = 2 * rows - 16 - start
        b0 = mirrored(back)
        b1 = mirrored(back + 1)
        chunk_cos = twist_ref[0, pl.ds(chunk, 1), :]
        chunk_sin = twist_ref[1, pl.ds(chunk, 1), :]
        cosine = base_cos * chunk_cos - base_sin * chunk_sin
        sine = base_sin * chunk_cos + base_cos * chunk_sin
        odd_real = a1 + b1
        odd_imag = b0 - a0
        out_real = (a0 + b0) + cosine * odd_real + sine * odd_imag
        out_imag = (a1 - b1) + cosine * odd_imag - sine * odd_real
        place = pl.ds(pl.multiple_of(chunk * 8 + 8, 8), 8)
        real[place, :] = out_real * half_scale
        imag[place, :] = out_imag * half_scale
        return 0

    group = 16
    lowest = jnp.maximum(device * (block_rows // 8) - 1, 0) // (8 * group)
    highest = jnp.minimum(((device + 1) * block_rows + 8 * group) // (8 * group), rows // (8 * group))

    def unpack_group(i, _):
        for j in range(group):
            unpack(i * group + j, 0)
        return 0

    lax.fori_loop(lowest, highest, unpack_group, 0)

    wide_lanes = lax.broadcasted_iota(jnp.int32, (segments, LANES), 1)
    def make_windows(n, stride):
        if stride == 8:
            first_row = device * block_rows + 8
        else:
            first_row = map_ref[n, 0] * block_rows + (map_ref[n, 2] >> 7) + 8
        for o in range(8):
            ahead = 2 * stride * 8 * o - LANES // 2
            skip, shift = ahead // LANES, ahead % LANES
            for c, source in enumerate((real, imag)):
                tiles = [
                    source[pl.ds(first_row + (skip + j), segments, stride=stride), :]
                    for j in range(3 if shift else 2)
                ]
                for half in range(2):
                    if shift:
                        tile = jnp.where(wide_lanes >= shift, tiles[half], tiles[half + 1])
                        tile = pltpu.roll(tile.astype(BF16), LANES - shift, 1)
                    else:
                        tile = tiles[half].astype(BF16)
                    at = (2 * c + half) * LANES
                    windows[n][o * segments : (o + 1) * segments, at : at + LANES] = tile

    def add_up(first, last):
        for t in range(first, last):
            for h in range(2):
                shared = {
                    n: [planes[t // share][n][t % share, h, pl.ds(c, LANES // 8, stride=stride), :] for c in range(stride + 1)]
                    for n, stride in enumerate(strides)
                    if stride <= 2
                }
                for b in range(8):
                    total = None
                    for n, stride in enumerate(strides):
                        plane = planes[t // share][n].at[t % share, h]
                        if stride == 8:
                            value = plane[pl.ds(b, LANES // 8, stride=8), :]
                        elif stride <= 2:
                            first = (map_ref[n, 3] + b * stride) >> 3
                            value = shared[n][0]
                            for c in range(1, stride + 1):
                                value = jnp.where(first == c, shared[n][c], value)
                        else:
                            first = (map_ref[n, 3] + b * stride) >> 3
                            value = plane[pl.ds(first, LANES // 8, stride=stride), :]
                        total = value if total is None else total + value
                    acc[(2 * t + h) % 2, pl.ds(b, LANES // 8, stride=8), :] = total * 0.125
                turned = acc[(2 * t + h) % 2].T
                for o in range(4):
                    flat[t % 2, pl.ds(4 * h + o, segments, stride=8), :] = turned[o * segments : (o + 1) * segments, :]
            for m in range(segments):
                out_ref[pl.ds(8 * templates * m + t, 8, stride=templates), :] = flat[t % 2, 8 * m : 8 * m + 8, :]

    for g in range(groups):
        own = weights[2 * g * share * LANES : 2 * (g + 1) * share * LANES, :]
        own = own.reshape(2 * share, LANES, 4 * LANES)
        for n, stride in enumerate(strides):
            height = planes[g][n].shape[2]
            if g == 0:
                make_windows(n, stride)
            amps = lax.dot_general(
                own[:, :height].reshape(2 * share * height, 4 * LANES),
                windows[n][...],
                (((1,), (1,)), ((), ())),
                preferred_element_type=F32,
            ).reshape(share, 2, height, 2 * 4 * segments)
            for t in range(share):
                plane = amps[t, 0] * amps[t, 0] + amps[t, 1] * amps[t, 1]
                for h in range(2):
                    planes[g][n][t, h] = plane[:, h * 4 * segments : (h + 1) * 4 * segments]
        if g:
            add_up((g - 1) * share, g * share)
    add_up((groups - 1) * share, templates)


def search(pieces, layout, weights, base, twist, harm_map, place, blocks, templates):
    block_rows = pieces[0].shape[0]
    rows = block_rows * blocks
    strides = STRIDE_TABLE + (8,)
    segments = block_rows // 8
    heights = [min(LANES, 16 * stride + 16) for stride in strides]
    smem = pl.BlockSpec(memory_space=pltpu.SMEM)
    vmem = pl.BlockSpec(memory_space=pltpu.VMEM)
    scratch = [
        ((2 * rows + 16, LANES), F32),
        ((rows + 16, LANES), F32),
        ((rows + 16, LANES), F32),
        ((2, LANES, 4 * segments), F32),
        ((2, block_rows, LANES), F32),
    ] + len(strides) * [((block_rows, 4 * LANES), BF16)] + 2 * [((templates // 2, 2, height, block_rows // 2), F32) for height in heights]
    used = sum(math.prod(shape) * jnp.dtype(kind).itemsize for shape, kind in scratch)
    return pl.pallas_call(
        functools.partial(search_kernel, strides, (block_rows, blocks, templates, layout)),
        out_shape=jax.ShapeDtypeStruct((block_rows * templates, LANES), F32),
        in_specs=[smem, smem] + [vmem] * (3 + len(pieces)),
        out_specs=vmem,
        scratch_shapes=[
            *[pltpu.VMEM(shape, kind) for shape, kind in scratch],
        ],
        compiler_params=pltpu.CompilerParams(vmem_limit_bytes=used + 12 * 2**20),
        name="search",
    )(
        place,
        harm_map,
        base,
        twist,
        *pieces,
        weights,
    )


def from_across(value, pair):
    blocks, peers = lax.axis_size("bins"), lax.axis_size("fdot")
    pairs = [
        (peers * d + f, peers * (d ^ (pair + 1 - (f >> 1) % 2)) + f)
        for d in range(blocks)
        for f in range(peers)
    ]
    return lax.ppermute(value, ("bins", "fdot"), pairs)


def body(spectrum, bank, fdot_index, harm_map):
    block_len = spectrum.shape[1]
    block_rows = block_len // LANES
    blocks = lax.axis_size("bins")
    templates = fdot_index.shape[0]
    device = lax.axis_index("bins")
    peer = lax.axis_index("fdot")
    part = peer & 1
    place = jnp.stack([device, part, (peer >> 1) & 1]).astype(jnp.int32)
    packed = spectrum.reshape(2, block_rows, LANES).transpose(1, 0, 2).reshape(2 * block_rows, LANES)
    mine = lax.dynamic_slice(packed, (part * block_rows, jnp.int32(0)), (block_rows, LANES))
    far = [from_across(mine, pair) for pair in range(2, blocks, 2)]
    steps = harm_map.reshape(-1, 4)
    fdot_index, steps, place = lax.optimization_barrier((fdot_index, steps, place))
    weights, base, twist = template_rows(bank, fdot_index, block_rows * blocks)
    sent, base = lax.optimization_barrier((mine, base))
    held = [sent, from_partner(sent, "bins", 1)]
    layout = [(0, 0), (1, 0)]
    for value, pair in zip(far, range(2, blocks, 2)):
        value = lax.optimization_barrier((value, base))[0]
        held += [value, from_partner(value, "fdot", 2)]
        layout += [(pair, 1), (pair, 0)]
    passed = [from_partner(value, "fdot", 1) for value in held]
    out = search(held + passed, layout, weights, base, twist, steps, place, blocks, templates)
    return out.reshape(block_rows, templates, LANES).transpose(1, 0, 2).reshape(templates, block_len)


def solution(mesh):
    placed = (P(None, ("groups", "bins")), P(), P("fdot"), P(None, "bins", None))
    return jax.shard_map(
        body, mesh=mesh, in_specs=placed, out_specs=P("fdot", ("groups", "bins")), check_vma=False
    )
```

```python
import functools
import math

import jax
import jax.numpy as jnp
from jax import lax
from jax.experimental import pallas as pl
from jax.experimental.pallas import tpu as pltpu
from jax.sharding import PartitionSpec as P

LANES = 128
STRIDE_TABLE = (4, 2, 6, 1, 3, 5, 7)
F32 = jnp.float32
BF16 = jnp.bfloat16
GROUPS = 2


def from_partner(value, axis, mask):
    pairs = [(source, source ^ mask) for source in range(lax.axis_size(axis))]
    return lax.ppermute(value, axis, pairs)


def template_kernel(
    step, groups, index_hbm, bank_hbm, out_ref, extra_ref, base_ref, twist_ref, index_ref, bank_ref, sem
):
    pairs = ((index_hbm, index_ref), (bank_hbm, bank_ref))
    copies = [pltpu.make_async_copy(source, to, sem.at[i]) for i, (source, to) in enumerate(pairs)]
    for copy in copies:
        copy.start()

    row_ids = lax.broadcasted_iota(jnp.int32, (8, LANES), 0)
    lanes = lax.broadcasted_iota(jnp.int32, (8, LANES), 1)
    fine = (row_ids * LANES + lanes).astype(F32) * F32(step)
    base_ref[0:8, :] = jnp.cos(fine)
    base_ref[8:16, :] = jnp.sin(fine)
    chunks = twist_ref.shape[1]
    coarse = lax.broadcasted_iota(jnp.int32, (chunks, LANES), 0).astype(F32)
    coarse = coarse * F32(step * 8 * LANES)
    twist_ref[0] = jnp.cos(coarse)
    twist_ref[1] = jnp.sin(coarse)

    copies[0].wait()
    copies[1].wait()
    zeros = jnp.zeros((1, LANES), F32)

    def banded(row):
        wide = jnp.broadcast_to(jnp.concatenate([row, zeros], axis=1), (LANES, 2 * LANES))
        return pltpu.roll(wide, 0, 1, stride=1, stride_axis=0)

    tables = []
    for t in range(index_ref.shape[0]):
        taps = bank_ref[index_ref[t]].astype(F32)
        real = banded(taps[0:1])
        imag = banded(taps[1:2])
        top, low = 2 * t * LANES, (2 * t + 1) * LANES
        out_ref[top : top + LANES, : 2 * LANES] = real.astype(BF16)
        out_ref[top : top + LANES, 2 * LANES :] = (-imag).astype(BF16)
        out_ref[low : low + LANES, : 2 * LANES] = imag.astype(BF16)
        out_ref[low : low + LANES, 2 * LANES :] = real.astype(BF16)
        tables.append((real, imag))

    count = len(tables)
    for n, stride in enumerate(STRIDE_TABLE):
        at = slice(16 * stride, 16 * stride + 1)
        for g in range(groups):
            some = tables[g * count // groups : (g + 1) * count // groups]
            pad = [jnp.zeros((8 - len(some), 2 * LANES), F32)] if len(some) < 8 else []
            real = jnp.concatenate([value[0][at] for value in some] + pad)
            imag = jnp.concatenate([value[1][at] for value in some] + pad)
            low = 16 * (groups * n + g)
            extra_ref[low : low + 16, : 2 * LANES] = jnp.concatenate([real, imag]).astype(BF16)
            extra_ref[low : low + 16, 2 * LANES :] = jnp.concatenate([-imag, real]).astype(BF16)


def template_rows(bank, fdot_index, rows):
    count = fdot_index.shape[0]
    taps = bank.shape[2]
    height = 2 * count * taps
    vmem = pl.BlockSpec(memory_space=pltpu.VMEM)
    return pl.pallas_call(
        functools.partial(template_kernel, math.pi / (rows * LANES), GROUPS),
        in_specs=[pl.BlockSpec(memory_space=pltpu.HBM)] * 2,
        out_specs=[vmem] * 4,
        out_shape=[
            jax.ShapeDtypeStruct((height, 4 * taps), BF16),
            jax.ShapeDtypeStruct((16 * GROUPS * len(STRIDE_TABLE), 4 * taps), BF16),
            jax.ShapeDtypeStruct((16, LANES), F32),
            jax.ShapeDtypeStruct((2, rows // 8, LANES), F32),
        ],
        scratch_shapes=[
            pltpu.SMEM(fdot_index.shape, jnp.int32),
            pltpu.VMEM(bank.shape, BF16),
            pltpu.SemaphoreType.DMA((2,)),
        ],
        cost_estimate=pl.CostEstimate(
            flops=4 * height * taps, bytes_accessed=8 * height * taps, transcendentals=0
        ),
        compiler_params=pltpu.CompilerParams(vmem_limit_bytes=16 * 2**20),
        name="template_rows",
    )(fdot_index, bank)


def search_kernel(strides, sizes, phase_hbm, base_ref, twist_ref, *refs):
    block_rows, blocks, templates, layout = sizes
    pieces = refs[: 2 * len(layout)]
    weights, extra, out_hbm, raw, real, imag, acc, flat, ready, phase_ref, out_sem, *more = refs[2 * len(layout) :]
    windows = more[: len(strides)]
    more = more[len(strides) :]
    groups = GROUPS
    share = templates // groups
    planes = [more[g * len(strides) : (g + 1) * len(strides)] for g in range(groups)]
    rows = block_rows * blocks
    total_bins = rows * LANES
    segments = block_rows // 8
    device = lax.axis_index("bins")
    peer = lax.axis_index("fdot")
    part = peer & 1
    column = (peer >> 1) & 1
    phase_copy = pltpu.make_async_copy(phase_hbm, phase_ref, out_sem.at[0])
    phase_copy.start()

    sums = [jnp.zeros((8, LANES), F32)] * 4
    for i, source in enumerate(pieces):
        pair, cross = layout[i % len(layout)]
        mask = pair + (1 - column if cross else column) if pair > 1 else pair
        half = part if i < len(layout) else 1 - part
        start = pl.multiple_of((device ^ mask) * (2 * block_rows) + half * block_rows, block_rows)
        for j in range(block_rows // 8):
            tile = source[8 * j : 8 * j + 8, :]
            raw[pl.ds(start + 8 * j, 8), :] = tile
            if j:
                sums[j % 4] = sums[j % 4] + tile * tile
    raw[2 * rows : 2 * rows + 16, :] = raw[0:16, :]
    row_ids = lax.broadcasted_iota(jnp.int32, (8, LANES), 0)
    lanes = lax.broadcasted_iota(jnp.int32, (8, LANES), 1)
    zero_tile = jnp.zeros((8, LANES), F32)
    half_scale = zero_tile + 0.001
    first_tile = raw[0:8, :]
    at_zero = (row_ids < 2) & (lanes == 0)
    zero_bin = jnp.sum(jnp.where(at_zero, first_tile, 0.0), keepdims=True)
    first_tile = jnp.where(at_zero, 0.0, first_tile)
    sums[0] = sums[0] + first_tile * first_tile
    for j in range(1, 2 * blocks):
        tile = raw[j * block_rows : j * block_rows + 8, :]
        sums[j % 4] = sums[j % 4] + tile * tile
    power = jnp.sum((sums[0] + sums[1]) + (sums[2] + sums[3]), keepdims=True)
    mean = jnp.broadcast_to((power + zero_bin * zero_bin) * (1.0 / total_bins) + 1e-06, (8, LANES))
    scale = lax.rsqrt(mean)
    scale = scale * (1.5 - 0.5 * mean * scale * scale)
    half_scale = 0.5 * scale

    base_cos = base_ref[0:8, :]
    base_sin = base_ref[8:16, :]
    mirror_lane = (LANES - lanes) & (LANES - 1)
    mirror_row = 7 - row_ids
    real[0:8, :] = zero_tile
    imag[0:8, :] = zero_tile
    real[rows + 8 : rows + 16, :] = zero_tile
    imag[rows + 8 : rows + 16, :] = zero_tile

    def mirrored(start):
        near = raw[pl.ds(start + 2, 8, stride=2), :]
        far = raw[pl.ds(start, 8, stride=2), :]
        tile = jnp.where(lanes == 0, near, far)
        tile = jnp.take_along_axis(tile, mirror_lane, axis=1, mode="promise_in_bounds")
        return jnp.take_along_axis(tile, mirror_row, axis=0, mode="promise_in_bounds")

    def unpack(chunk, _):
        start = chunk * 16
        a0 = raw[pl.ds(start, 8, stride=2), :]
        a1 = raw[pl.ds(start + 1, 8, stride=2), :]
        back = 2 * rows - 16 - start
        b0 = mirrored(back)
        b1 = mirrored(back + 1)
        chunk_cos = twist_ref[0, pl.ds(chunk, 1), :]
        chunk_sin = twist_ref[1, pl.ds(chunk, 1), :]
        cosine = base_cos * chunk_cos - base_sin * chunk_sin
        sine = base_sin * chunk_cos + base_cos * chunk_sin
        odd_real = a1 + b1
        odd_imag = b0 - a0
        out_real = (a0 + b0) + cosine * odd_real + sine * odd_imag
        out_imag = (a1 - b1) + cosine * odd_imag - sine * odd_real
        place = pl.ds(pl.multiple_of(chunk * 8 + 8, 8), 8)
        real[place, :] = out_real * half_scale
        imag[place, :] = out_imag * half_scale
        return 0

    group = 16
    lowest = jnp.maximum(device * (block_rows // 8) - 1, 0) // (8 * group)
    highest = jnp.minimum(((device + 1) * block_rows + 8 * group) // (8 * group), rows // (8 * group))

    def unpack_group(i, _):
        for j in range(group):
            unpack(i * group + j, 0)
        return 0

    lax.fori_loop(lowest, highest, unpack_group, 0)

    wide_lanes = lax.broadcasted_iota(jnp.int32, (segments, LANES), 1)
    def make_windows(n, stride):
        first_row = device * (block_rows * stride // 8) + 8
        for o in range(8):
            ahead = 2 * stride * 8 * o - LANES // 2
            skip, shift = ahead // LANES, ahead % LANES
            for c, source in enumerate((real, imag)):
                tiles = [
                    source[pl.ds(first_row + (skip + j), segments, stride=stride), :]
                    for j in range(3 if shift else 2)
                ]
                for half in range(2):
                    if shift:
                        tile = jnp.where(wide_lanes >= shift, tiles[half], tiles[half + 1])
                        tile = pltpu.roll(tile.astype(BF16), LANES - shift, 1)
                    else:
                        tile = tiles[half].astype(BF16)
                    at = (2 * c + half) * LANES
                    windows[n][o * segments : (o + 1) * segments, at : at + LANES] = tile

    def add_up(t, h):
        total = [None] * 8
        for n, stride in enumerate(strides):
            plane = planes[t // share][n].at[t % share, h]
            if stride == 8:
                values = [plane[pl.ds(b, LANES // 8, stride=8), :] for b in range(8)]
            else:
                starts = [plane[pl.ds(c, LANES // 8, stride=stride), :] for c in range(stride + 1)]
                values = []
                for b in range(8):
                    least = stride * b // 8
                    ahead = phase_ref[n] + stride * b >= 8 * (least + 1)
                    values.append(jnp.where(ahead, starts[least + 1], starts[least]))
            total = values if n == 0 else [x + y for x, y in zip(total, values)]
        for b in range(8):
            acc[(2 * t + h) % 2, pl.ds(b, LANES // 8, stride=8), :] = total[b] * 0.125
        turned = acc[(2 * t + h) % 2].T
        for o in range(4):
            flat[t, pl.ds(4 * h + o, segments, stride=8), :] = turned[o * segments : (o + 1) * segments, :]

    phase_copy.wait()
    for g in range(groups):
        own = weights[2 * g * share * LANES : 2 * (g + 1) * share * LANES, :]
        own = own.reshape(2 * share, LANES, 4 * LANES)
        for n, stride in enumerate(strides):
            if g == 0:
                make_windows(n, stride)
            height = 16 * stride
            lhs = own[:, :height].reshape(2 * share * height, 4 * LANES)
            if stride < 8:
                low = 16 * (groups * n + g)
                lhs = jnp.concatenate([lhs, extra[low : low + 16, :]])
            amps = lax.dot_general(
                lhs, windows[n][...], (((1,), (1,)), ((), ())), preferred_element_type=F32
            )
            for t in range(share):
                top = 2 * t * height
                plane = amps[top : top + height] ** 2 + amps[top + height : top + 2 * height] ** 2
                for h in range(2):
                    planes[g][n][t, h, :height] = plane[:, h * 4 * segments : (h + 1) * 4 * segments]
            if stride < 8:
                top = 2 * share * height
                last = amps[top : top + 8] ** 2 + amps[top + 8 : top + 16] ** 2
                for t in range(share):
                    for h in range(2):
                        planes[g][n][t, h, height : height + 1] = last[
                            t : t + 1, h * 4 * segments : (h + 1) * 4 * segments
                        ]
            if g:
                units = range(2 * share * n // len(strides), 2 * share * (n + 1) // len(strides))
                for unit in units:
                    add_up((g - 1) * share + unit // 2, unit % 2)
    for unit in range(2 * share):
        add_up((groups - 1) * share + unit // 2, unit % 2)
    parts = out_sem.shape[0]
    span = block_rows * templates // parts
    copies = []
    for i in range(parts):
        for m in range(i * segments // parts, (i + 1) * segments // parts):
            for t in range(templates):
                ready[pl.ds(8 * templates * m + t, 8, stride=templates), :] = flat[t, 8 * m : 8 * m + 8, :]
        done = pl.ds(i * span, span)
        copies.append(pltpu.make_async_copy(ready.at[done, :], out_hbm.at[done, :], out_sem.at[i]))
        copies[-1].start()
    for copy in copies:
        copy.wait()


def search(pieces, layout, weights, extra, base, twist, phases, blocks, templates):
    block_rows = pieces[0].shape[0]
    rows = block_rows * blocks
    strides = STRIDE_TABLE + (8,)
    segments = block_rows // 8
    heights = [min(LANES, 16 * stride + 8) for stride in strides]
    vmem = pl.BlockSpec(memory_space=pltpu.VMEM)
    scratch = [
        ((2 * rows + 16, LANES), F32),
        ((rows + 16, LANES), F32),
        ((rows + 16, LANES), F32),
        ((2, LANES, 4 * segments), F32),
        ((templates, block_rows, LANES), F32),
        ((block_rows * templates, LANES), F32),
    ] + len(strides) * [((block_rows, 4 * LANES), BF16)] + GROUPS * [((templates // GROUPS, 2, height, block_rows // 2), F32) for height in heights]
    used = sum(math.prod(shape) * jnp.dtype(kind).itemsize for shape, kind in scratch)
    return pl.pallas_call(
        functools.partial(search_kernel, strides, (block_rows, blocks, templates, layout)),
        out_shape=jax.ShapeDtypeStruct((block_rows * templates, LANES), F32),
        in_specs=[pl.BlockSpec(memory_space=pl.ANY)] + [vmem] * (4 + len(pieces)),
        out_specs=pl.BlockSpec(memory_space=pltpu.HBM),
        scratch_shapes=[
            *[pltpu.VMEM(shape, kind) for shape, kind in scratch[:6]],
            pltpu.SMEM(phases.shape, jnp.int32),
            pltpu.SemaphoreType.DMA((4,)),
            *[pltpu.VMEM(shape, kind) for shape, kind in scratch[6:]],
        ],
        compiler_params=pltpu.CompilerParams(vmem_limit_bytes=used + 12 * 2**20),
        name="search",
    )(
        phases,
        base,
        twist,
        *pieces,
        weights,
        extra,
    )


def from_across(value, pair):
    blocks, peers = lax.axis_size("bins"), lax.axis_size("fdot")
    pairs = [
        (peers * d + f, peers * (d ^ (pair + 1 - (f >> 1) % 2)) + f)
        for d in range(blocks)
        for f in range(peers)
    ]
    return lax.ppermute(value, ("bins", "fdot"), pairs)


def body(spectrum, bank, fdot_index, harm_map):
    block_len = spectrum.shape[1]
    block_rows = block_len // LANES
    blocks = lax.axis_size("bins")
    templates = fdot_index.shape[0]
    part = lax.axis_index("fdot") & 1
    packed = spectrum.reshape(2, block_rows, LANES).transpose(1, 0, 2).reshape(2 * block_rows, LANES)
    mine = lax.dynamic_slice(packed, (part * block_rows, jnp.int32(0)), (block_rows, LANES))
    far = [from_across(mine, pair) for pair in range(2, blocks, 2)]
    fdot_index, phases = lax.optimization_barrier((fdot_index, harm_map[:, 0, 3]))
    weights, extra, base, twist = template_rows(bank, fdot_index, block_rows * blocks)
    sent, base = lax.optimization_barrier((mine, base))
    held = [sent, from_partner(sent, "bins", 1)]
    layout = [(0, 0), (1, 0)]
    for value, pair in zip(far, range(2, blocks, 2)):
        value = lax.optimization_barrier((value, base))[0]
        held += [value, from_partner(value, "fdot", 2)]
        layout += [(pair, 1), (pair, 0)]
    passed = [from_partner(value, "fdot", 1) for value in held]
    out = search(held + passed, layout, weights, extra, base, twist, phases, blocks, templates)
    return out.reshape(block_rows, templates, LANES).transpose(1, 0, 2).reshape(templates, block_len)


def solution(mesh):
    placed = (P(None, ("groups", "bins")), P(), P("fdot"), P(None, "bins", None))
    return jax.shard_map(
        body, mesh=mesh, in_specs=placed, out_specs=P("fdot", ("groups", "bins")), check_vma=False
    )
```

```python
import functools
import math

import jax
import jax.numpy as jnp
from jax import lax
from jax.experimental import pallas as pl
from jax.experimental.pallas import tpu as pltpu
from jax.sharding import PartitionSpec as P

LANES = 128
STRIDE_TABLE = (4, 2, 6, 1, 3, 5, 7)
F32 = jnp.float32
BF16 = jnp.bfloat16
GROUPS = 2


def from_partner(value, axis, mask):
    pairs = [(source, source ^ mask) for source in range(lax.axis_size(axis))]
    return lax.ppermute(value, axis, pairs)


def template_kernel(
    step, groups, index_hbm, bank_hbm, out_ref, extra_ref, base_ref, twist_ref, index_ref, bank_ref, sem
):
    pairs = ((index_hbm, index_ref), (bank_hbm, bank_ref))
    copies = [pltpu.make_async_copy(source, to, sem.at[i]) for i, (source, to) in enumerate(pairs)]
    for copy in copies:
        copy.start()

    row_ids = lax.broadcasted_iota(jnp.int32, (8, LANES), 0)
    lanes = lax.broadcasted_iota(jnp.int32, (8, LANES), 1)
    fine = (row_ids * LANES + lanes).astype(F32) * F32(step)
    base_ref[0:8, :] = jnp.cos(fine)
    base_ref[8:16, :] = jnp.sin(fine)
    chunks = twist_ref.shape[1]
    coarse = lax.broadcasted_iota(jnp.int32, (chunks, LANES), 0).astype(F32)
    coarse = coarse * F32(step * 8 * LANES)
    twist_ref[0] = jnp.cos(coarse)
    twist_ref[1] = jnp.sin(coarse)

    copies[0].wait()
    copies[1].wait()
    zeros = jnp.zeros((1, LANES), F32)

    def banded(row):
        wide = jnp.broadcast_to(jnp.concatenate([row, zeros], axis=1), (LANES, 2 * LANES))
        return pltpu.roll(wide, 0, 1, stride=1, stride_axis=0)

    tables = []
    for t in range(index_ref.shape[0]):
        taps = bank_ref[index_ref[t]].astype(F32)
        real = banded(taps[0:1])
        imag = banded(taps[1:2])
        top, low = 2 * t * LANES, (2 * t + 1) * LANES
        out_ref[top : top + LANES, : 2 * LANES] = real.astype(BF16)
        out_ref[top : top + LANES, 2 * LANES :] = (-imag).astype(BF16)
        out_ref[low : low + LANES, : 2 * LANES] = imag.astype(BF16)
        out_ref[low : low + LANES, 2 * LANES :] = real.astype(BF16)
        tables.append((real, imag))

    count = len(tables)
    for n, stride in enumerate(STRIDE_TABLE):
        at = slice(16 * stride, 16 * stride + 1)
        for g in range(groups):
            some = tables[g * count // groups : (g + 1) * count // groups]
            pad = [jnp.zeros((8 - len(some), 2 * LANES), F32)] if len(some) < 8 else []
            real = jnp.concatenate([value[0][at] for value in some] + pad)
            imag = jnp.concatenate([value[1][at] for value in some] + pad)
            low = 16 * (groups * n + g)
            extra_ref[low : low + 16, : 2 * LANES] = jnp.concatenate([real, imag]).astype(BF16)
            extra_ref[low : low + 16, 2 * LANES :] = jnp.concatenate([-imag, real]).astype(BF16)


def template_rows(bank, fdot_index, rows):
    count = fdot_index.shape[0]
    taps = bank.shape[2]
    height = 2 * count * taps
    vmem = pl.BlockSpec(memory_space=pltpu.VMEM)
    return pl.pallas_call(
        functools.partial(template_kernel, math.pi / (rows * LANES), GROUPS),
        in_specs=[pl.BlockSpec(memory_space=pltpu.HBM)] * 2,
        out_specs=[vmem] * 4,
        out_shape=[
            jax.ShapeDtypeStruct((height, 4 * taps), BF16),
            jax.ShapeDtypeStruct((16 * GROUPS * len(STRIDE_TABLE), 4 * taps), BF16),
            jax.ShapeDtypeStruct((16, LANES), F32),
            jax.ShapeDtypeStruct((2, rows // 8, LANES), F32),
        ],
        scratch_shapes=[
            pltpu.SMEM(fdot_index.shape, jnp.int32),
            pltpu.VMEM(bank.shape, BF16),
            pltpu.SemaphoreType.DMA((2,)),
        ],
        cost_estimate=pl.CostEstimate(
            flops=4 * height * taps, bytes_accessed=8 * height * taps, transcendentals=0
        ),
        compiler_params=pltpu.CompilerParams(vmem_limit_bytes=16 * 2**20),
        name="template_rows",
    )(fdot_index, bank)


def search_kernel(strides, sizes, phase_hbm, base_ref, twist_ref, *refs):
    block_rows, blocks, templates, layout = sizes
    pieces = refs[: 2 * len(layout)]
    weights, extra, out_hbm, raw, real, imag, acc, flat, phase_ref, out_sem, *more = refs[2 * len(layout) :]
    windows = more[: len(strides)]
    more = more[len(strides) :]
    groups = GROUPS
    share = templates // groups
    planes = [more[g * len(strides) : (g + 1) * len(strides)] for g in range(groups)]
    rows = block_rows * blocks
    total_bins = rows * LANES
    segments = block_rows // 8
    device = lax.axis_index("bins")
    peer = lax.axis_index("fdot")
    part = peer & 1
    column = (peer >> 1) & 1
    phase_copy = pltpu.make_async_copy(phase_hbm, phase_ref, out_sem.at[0])
    phase_copy.start()

    sums = [jnp.zeros((8, LANES), F32)] * 4
    for i, source in enumerate(pieces):
        pair, cross = layout[i % len(layout)]
        mask = pair + (1 - column if cross else column) if pair > 1 else pair
        half = part if i < len(layout) else 1 - part
        start = pl.multiple_of((device ^ mask) * (2 * block_rows) + half * block_rows, block_rows)
        for j in range(block_rows // 8):
            tile = source[8 * j : 8 * j + 8, :]
            raw[pl.ds(start + 8 * j, 8), :] = tile
            if j:
                sums[j % 4] = sums[j % 4] + tile * tile
    raw[2 * rows : 2 * rows + 16, :] = raw[0:16, :]
    row_ids = lax.broadcasted_iota(jnp.int32, (8, LANES), 0)
    lanes = lax.broadcasted_iota(jnp.int32, (8, LANES), 1)
    zero_tile = jnp.zeros((8, LANES), F32)
    half_scale = zero_tile + 0.001
    first_tile = raw[0:8, :]
    at_zero = (row_ids < 2) & (lanes == 0)
    zero_bin = jnp.sum(jnp.where(at_zero, first_tile, 0.0), keepdims=True)
    first_tile = jnp.where(at_zero, 0.0, first_tile)
    sums[0] = sums[0] + first_tile * first_tile
    for j in range(1, 2 * blocks):
        tile = raw[j * block_rows : j * block_rows + 8, :]
        sums[j % 4] = sums[j % 4] + tile * tile
    power = jnp.sum((sums[0] + sums[1]) + (sums[2] + sums[3]), keepdims=True)
    mean = jnp.broadcast_to((power + zero_bin * zero_bin) * (1.0 / total_bins) + 1e-06, (8, LANES))
    scale = lax.rsqrt(mean)
    scale = scale * (1.5 - 0.5 * mean * scale * scale)
    half_scale = 0.5 * scale

    base_cos = base_ref[0:8, :]
    base_sin = base_ref[8:16, :]
    mirror_lane = (LANES - lanes) & (LANES - 1)
    mirror_row = 7 - row_ids
    real[0:8, :] = zero_tile
    imag[0:8, :] = zero_tile
    real[rows + 8 : rows + 16, :] = zero_tile
    imag[rows + 8 : rows + 16, :] = zero_tile

    def mirrored(start):
        near = raw[pl.ds(start + 2, 8, stride=2), :]
        far = raw[pl.ds(start, 8, stride=2), :]
        tile = jnp.where(lanes == 0, near, far)
        tile = jnp.take_along_axis(tile, mirror_lane, axis=1, mode="promise_in_bounds")
        return jnp.take_along_axis(tile, mirror_row, axis=0, mode="promise_in_bounds")

    def unpack(chunk, _):
        start = chunk * 16
        a0 = raw[pl.ds(start, 8, stride=2), :]
        a1 = raw[pl.ds(start + 1, 8, stride=2), :]
        back = 2 * rows - 16 - start
        b0 = mirrored(back)
        b1 = mirrored(back + 1)
        chunk_cos = twist_ref[0, pl.ds(chunk, 1), :]
        chunk_sin = twist_ref[1, pl.ds(chunk, 1), :]
        cosine = base_cos * chunk_cos - base_sin * chunk_sin
        sine = base_sin * chunk_cos + base_cos * chunk_sin
        odd_real = a1 + b1
        odd_imag = b0 - a0
        out_real = (a0 + b0) + cosine * odd_real + sine * odd_imag
        out_imag = (a1 - b1) + cosine * odd_imag - sine * odd_real
        place = pl.ds(pl.multiple_of(chunk * 8 + 8, 8), 8)
        real[place, :] = out_real * half_scale
        imag[place, :] = out_imag * half_scale
        return 0

    group = 16
    lowest = jnp.maximum(device * (block_rows // 8) - 1, 0) // (8 * group)
    highest = jnp.minimum(((device + 1) * block_rows + 8 * group) // (8 * group), rows // (8 * group))

    def unpack_group(i, _):
        for j in range(group):
            unpack(i * group + j, 0)
        return 0

    lax.fori_loop(lowest, highest, unpack_group, 0)

    wide_lanes = lax.broadcasted_iota(jnp.int32, (segments, LANES), 1)
    def make_windows(n, stride):
        first_row = device * (block_rows * stride // 8) + 8
        for o in range(8):
            ahead = 2 * stride * 8 * o - LANES // 2
            skip, shift = ahead // LANES, ahead % LANES
            for c, source in enumerate((real, imag)):
                tiles = [
                    source[pl.ds(first_row + (skip + j), segments, stride=stride), :]
                    for j in range(3 if shift else 2)
                ]
                for half in range(2):
                    if shift:
                        tile = jnp.where(wide_lanes >= shift, tiles[half], tiles[half + 1])
                        tile = pltpu.roll(tile.astype(BF16), LANES - shift, 1)
                    else:
                        tile = tiles[half].astype(BF16)
                    at = (2 * c + half) * LANES
                    windows[n][o * segments : (o + 1) * segments, at : at + LANES] = tile

    copies = []

    def add_up(t, h):
        total = [None] * 8
        for n, stride in enumerate(strides):
            plane = planes[t // share][n].at[t % share, h]
            if stride == 8:
                values = [plane[pl.ds(b, LANES // 8, stride=8), :] for b in range(8)]
            else:
                starts = [plane[pl.ds(c, LANES // 8, stride=stride), :] for c in range(stride + 1)]
                values = []
                for b in range(8):
                    least = stride * b // 8
                    ahead = phase_ref[n] + stride * b >= 8 * (least + 1)
                    values.append(jnp.where(ahead, starts[least + 1], starts[least]))
            total = values if n == 0 else [x + y for x, y in zip(total, values)]
        for b in range(8):
            acc[(2 * t + h) % 2, pl.ds(b, LANES // 8, stride=8), :] = total[b] * 0.125
        turned = acc[(2 * t + h) % 2].T
        for o in range(4):
            flat[t, pl.ds(4 * h + o, segments, stride=8), :] = turned[o * segments : (o + 1) * segments, :]
        if h:
            copies.append(pltpu.make_async_copy(flat.at[t], out_hbm.at[:, t, :], out_sem.at[t]))
            copies[-1].start()

    phase_copy.wait()
    for g in range(groups):
        own = weights[2 * g * share * LANES : 2 * (g + 1) * share * LANES, :]
        own = own.reshape(2 * share, LANES, 4 * LANES)
        for n, stride in enumerate(strides):
            if g == 0:
                make_windows(n, stride)
            height = 16 * stride
            lhs = own[:, :height].reshape(2 * share * height, 4 * LANES)
            if stride < 8:
                low = 16 * (groups * n + g)
                lhs = jnp.concatenate([lhs, extra[low : low + 16, :]])
            amps = lax.dot_general(
                lhs, windows[n][...], (((1,), (1,)), ((), ())), preferred_element_type=F32
            )
            for t in range(share):
                top = 2 * t * height
                plane = amps[top : top + height] ** 2 + amps[top + height : top + 2 * height] ** 2
                for h in range(2):
                    planes[g][n][t, h, :height] = plane[:, h * 4 * segments : (h + 1) * 4 * segments]
            if stride < 8:
                top = 2 * share * height
                last = amps[top : top + 8] ** 2 + amps[top + 8 : top + 16] ** 2
                for t in range(share):
                    for h in range(2):
                        planes[g][n][t, h, height : height + 1] = last[
                            t : t + 1, h * 4 * segments : (h + 1) * 4 * segments
                        ]
            if g:
                units = range(2 * share * n // len(strides), 2 * share * (n + 1) // len(strides))
                for unit in units:
                    add_up((g - 1) * share + unit // 2, unit % 2)
    for unit in range(2 * share):
        add_up((groups - 1) * share + unit // 2, unit % 2)
    for copy in copies:
        copy.wait()


def search(pieces, layout, weights, extra, base, twist, phases, blocks, templates):
    block_rows = pieces[0].shape[0]
    rows = block_rows * blocks
    strides = STRIDE_TABLE + (8,)
    segments = block_rows // 8
    heights = [min(LANES, 16 * stride + 8) for stride in strides]
    vmem = pl.BlockSpec(memory_space=pltpu.VMEM)
    scratch = [
        ((2 * rows + 16, LANES), F32),
        ((rows + 16, LANES), F32),
        ((rows + 16, LANES), F32),
        ((2, LANES, 4 * segments), F32),
        ((templates, block_rows, LANES), F32),
    ] + len(strides) * [((block_rows, 4 * LANES), BF16)] + GROUPS * [((templates // GROUPS, 2, height, block_rows // 2), F32) for height in heights]
    used = sum(math.prod(shape) * jnp.dtype(kind).itemsize for shape, kind in scratch)
    return pl.pallas_call(
        functools.partial(search_kernel, strides, (block_rows, blocks, templates, layout)),
        out_shape=jax.ShapeDtypeStruct((block_rows, templates, LANES), F32),
        in_specs=[pl.BlockSpec(memory_space=pl.ANY)] + [vmem] * (4 + len(pieces)),
        out_specs=pl.BlockSpec(memory_space=pltpu.HBM),
        scratch_shapes=[
            *[pltpu.VMEM(shape, kind) for shape, kind in scratch[:5]],
            pltpu.SMEM(phases.shape, jnp.int32),
            pltpu.SemaphoreType.DMA((templates,)),
            *[pltpu.VMEM(shape, kind) for shape, kind in scratch[5:]],
        ],
        compiler_params=pltpu.CompilerParams(vmem_limit_bytes=used + 12 * 2**20),
        name="search",
    )(
        phases,
        base,
        twist,
        *pieces,
        weights,
        extra,
    )


def from_across(value, pair):
    blocks, peers = lax.axis_size("bins"), lax.axis_size("fdot")
    pairs = [
        (peers * d + f, peers * (d ^ (pair + 1 - (f >> 1) % 2)) + f)
        for d in range(blocks)
        for f in range(peers)
    ]
    return lax.ppermute(value, ("bins", "fdot"), pairs)


def body(spectrum, bank, fdot_index, harm_map):
    block_len = spectrum.shape[1]
    block_rows = block_len // LANES
    blocks = lax.axis_size("bins")
    templates = fdot_index.shape[0]
    part = lax.axis_index("fdot") & 1
    packed = spectrum.reshape(2, block_rows, LANES).transpose(1, 0, 2).reshape(2 * block_rows, LANES)
    mine = lax.dynamic_slice(packed, (part * block_rows, jnp.int32(0)), (block_rows, LANES))
    far = [from_across(mine, pair) for pair in range(2, blocks, 2)]
    fdot_index, phases = lax.optimization_barrier((fdot_index, harm_map[:, 0, 3]))
    weights, extra, base, twist = template_rows(bank, fdot_index, block_rows * blocks)
    sent, base = lax.optimization_barrier((mine, base))
    held = [sent, from_partner(sent, "bins", 1)]
    layout = [(0, 0), (1, 0)]
    for value, pair in zip(far, range(2, blocks, 2)):
        value = lax.optimization_barrier((value, base))[0]
        held += [value, from_partner(value, "fdot", 2)]
        layout += [(pair, 1), (pair, 0)]
    passed = [from_partner(value, "fdot", 1) for value in held]
    out = search(held + passed, layout, weights, extra, base, twist, phases, blocks, templates)
    return out.transpose(1, 0, 2).reshape(templates, block_len)


def solution(mesh):
    placed = (P(None, ("groups", "bins")), P(), P("fdot"), P(None, "bins", None))
    return jax.shard_map(
        body, mesh=mesh, in_specs=placed, out_specs=P("fdot", ("groups", "bins")), check_vma=False
    )
```

```python
import functools
import math

import jax
import jax.numpy as jnp
from jax import lax
from jax.experimental import pallas as pl
from jax.experimental.pallas import tpu as pltpu
from jax.sharding import PartitionSpec as P

LANES = 128
STRIDE_TABLE = (4, 2, 6, 1, 3, 5, 7)
F32 = jnp.float32
BF16 = jnp.bfloat16
GROUPS = 2


def from_partner(value, axis, mask):
    pairs = [(source, source ^ mask) for source in range(lax.axis_size(axis))]
    return lax.ppermute(value, axis, pairs)


def template_kernel(
    step, groups, index_hbm, bank_hbm, out_ref, extra_ref, base_ref, twist_ref, index_ref, bank_ref, sem
):
    pairs = ((index_hbm, index_ref), (bank_hbm, bank_ref))
    copies = [pltpu.make_async_copy(source, to, sem.at[i]) for i, (source, to) in enumerate(pairs)]
    for copy in copies:
        copy.start()

    row_ids = lax.broadcasted_iota(jnp.int32, (8, LANES), 0)
    lanes = lax.broadcasted_iota(jnp.int32, (8, LANES), 1)
    fine = (row_ids * LANES + lanes).astype(F32) * F32(step)
    base_ref[0:8, :] = jnp.cos(fine)
    base_ref[8:16, :] = jnp.sin(fine)
    chunks = twist_ref.shape[1]
    coarse = lax.broadcasted_iota(jnp.int32, (chunks, LANES), 0).astype(F32)
    coarse = coarse * F32(step * 8 * LANES)
    twist_ref[0] = jnp.cos(coarse)
    twist_ref[1] = jnp.sin(coarse)

    copies[0].wait()
    copies[1].wait()
    zeros = jnp.zeros((1, LANES), F32)

    def banded(row):
        wide = jnp.broadcast_to(jnp.concatenate([row, zeros], axis=1), (LANES, 2 * LANES))
        return pltpu.roll(wide, 0, 1, stride=1, stride_axis=0)

    tables = []
    for t in range(index_ref.shape[0]):
        taps = bank_ref[index_ref[t]].astype(F32)
        real = banded(taps[0:1])
        imag = banded(taps[1:2])
        top, low = 2 * t * LANES, (2 * t + 1) * LANES
        out_ref[top : top + LANES, : 2 * LANES] = real.astype(BF16)
        out_ref[top : top + LANES, 2 * LANES :] = (-imag).astype(BF16)
        out_ref[low : low + LANES, : 2 * LANES] = imag.astype(BF16)
        out_ref[low : low + LANES, 2 * LANES :] = real.astype(BF16)
        tables.append((real, imag))

    count = len(tables)
    for n, stride in enumerate(STRIDE_TABLE):
        at = slice(16 * stride, 16 * stride + 1)
        for g in range(groups):
            some = tables[g * count // groups : (g + 1) * count // groups]
            pad = [jnp.zeros((8 - len(some), 2 * LANES), F32)] if len(some) < 8 else []
            real = jnp.concatenate([value[0][at] for value in some] + pad)
            imag = jnp.concatenate([value[1][at] for value in some] + pad)
            low = 16 * (groups * n + g)
            extra_ref[low : low + 16, : 2 * LANES] = jnp.concatenate([real, imag]).astype(BF16)
            extra_ref[low : low + 16, 2 * LANES :] = jnp.concatenate([-imag, real]).astype(BF16)


def template_rows(bank, fdot_index, rows):
    count = fdot_index.shape[0]
    taps = bank.shape[2]
    height = 2 * count * taps
    vmem = pl.BlockSpec(memory_space=pltpu.VMEM)
    return pl.pallas_call(
        functools.partial(template_kernel, math.pi / (rows * LANES), GROUPS),
        in_specs=[pl.BlockSpec(memory_space=pltpu.HBM)] * 2,
        out_specs=[vmem] * 4,
        out_shape=[
            jax.ShapeDtypeStruct((height, 4 * taps), BF16),
            jax.ShapeDtypeStruct((16 * GROUPS * len(STRIDE_TABLE), 4 * taps), BF16),
            jax.ShapeDtypeStruct((16, LANES), F32),
            jax.ShapeDtypeStruct((2, rows // 8, LANES), F32),
        ],
        scratch_shapes=[
            pltpu.SMEM(fdot_index.shape, jnp.int32),
            pltpu.VMEM(bank.shape, BF16),
            pltpu.SemaphoreType.DMA((2,)),
        ],
        cost_estimate=pl.CostEstimate(
            flops=4 * height * taps, bytes_accessed=8 * height * taps, transcendentals=0
        ),
        compiler_params=pltpu.CompilerParams(vmem_limit_bytes=16 * 2**20),
        name="template_rows",
    )(fdot_index, bank)


def search_kernel(strides, sizes, phase_hbm, base_ref, twist_ref, *refs):
    block_rows, blocks, templates, layout = sizes
    pieces = refs[: 2 * len(layout)]
    weights, extra, out_hbm, raw, real, imag, acc, flat, phase_ref, out_sem, *more = refs[2 * len(layout) :]
    windows = more[: len(strides)]
    more = more[len(strides) :]
    groups = GROUPS
    share = templates // groups
    planes = [more[g * len(strides) : (g + 1) * len(strides)] for g in range(groups)]
    rows = block_rows * blocks
    total_bins = rows * LANES
    segments = block_rows // 8
    device = lax.axis_index("bins")
    peer = lax.axis_index("fdot")
    part = peer & 1
    column = (peer ^ (peer >> 1)) & 1
    phase_copy = pltpu.make_async_copy(phase_hbm, phase_ref, out_sem.at[0])
    phase_copy.start()

    sums = [jnp.zeros((8, LANES), F32)] * 4
    for i, source in enumerate(pieces):
        pair, cross = layout[i % len(layout)]
        mask = pair + (column if cross == (i >= len(layout)) else 1 - column) if pair > 1 else pair
        half = part if i < len(layout) else 1 - part
        start = pl.multiple_of((device ^ mask) * (2 * block_rows) + half * block_rows, block_rows)
        for j in range(block_rows // 8):
            tile = source[8 * j : 8 * j + 8, :]
            raw[pl.ds(start + 8 * j, 8), :] = tile
            if j:
                sums[j % 4] = sums[j % 4] + tile * tile
    raw[2 * rows : 2 * rows + 16, :] = raw[0:16, :]
    row_ids = lax.broadcasted_iota(jnp.int32, (8, LANES), 0)
    lanes = lax.broadcasted_iota(jnp.int32, (8, LANES), 1)
    zero_tile = jnp.zeros((8, LANES), F32)
    half_scale = zero_tile + 0.001
    first_tile = raw[0:8, :]
    at_zero = (row_ids < 2) & (lanes == 0)
    zero_bin = jnp.sum(jnp.where(at_zero, first_tile, 0.0), keepdims=True)
    first_tile = jnp.where(at_zero, 0.0, first_tile)
    sums[0] = sums[0] + first_tile * first_tile
    for j in range(1, 2 * blocks):
        tile = raw[j * block_rows : j * block_rows + 8, :]
        sums[j % 4] = sums[j % 4] + tile * tile
    power = jnp.sum((sums[0] + sums[1]) + (sums[2] + sums[3]), keepdims=True)
    mean = jnp.broadcast_to((power + zero_bin * zero_bin) * (1.0 / total_bins) + 1e-06, (8, LANES))
    scale = lax.rsqrt(mean)
    scale = scale * (1.5 - 0.5 * mean * scale * scale)
    half_scale = 0.5 * scale

    base_cos = base_ref[0:8, :]
    base_sin = base_ref[8:16, :]
    mirror_lane = (LANES - lanes) & (LANES - 1)
    mirror_row = 7 - row_ids
    real[0:8, :] = zero_tile
    imag[0:8, :] = zero_tile
    real[rows + 8 : rows + 16, :] = zero_tile
    imag[rows + 8 : rows + 16, :] = zero_tile

    def mirrored(start):
        near = raw[pl.ds(start + 2, 8, stride=2), :]
        far = raw[pl.ds(start, 8, stride=2), :]
        tile = jnp.where(lanes == 0, near, far)
        tile = jnp.take_along_axis(tile, mirror_lane, axis=1, mode="promise_in_bounds")
        return jnp.take_along_axis(tile, mirror_row, axis=0, mode="promise_in_bounds")

    def unpack(chunk, _):
        start = chunk * 16
        a0 = raw[pl.ds(start, 8, stride=2), :]
        a1 = raw[pl.ds(start + 1, 8, stride=2), :]
        back = 2 * rows - 16 - start
        b0 = mirrored(back)
        b1 = mirrored(back + 1)
        chunk_cos = twist_ref[0, pl.ds(chunk, 1), :]
        chunk_sin = twist_ref[1, pl.ds(chunk, 1), :]
        cosine = base_cos * chunk_cos - base_sin * chunk_sin
        sine = base_sin * chunk_cos + base_cos * chunk_sin
        odd_real = a1 + b1
        odd_imag = b0 - a0
        out_real = (a0 + b0) + cosine * odd_real + sine * odd_imag
        out_imag = (a1 - b1) + cosine * odd_imag - sine * odd_real
        place = pl.ds(pl.multiple_of(chunk * 8 + 8, 8), 8)
        real[place, :] = out_real * half_scale
        imag[place, :] = out_imag * half_scale
        return 0

    group = 16
    lowest = jnp.maximum(device * (block_rows // 8) - 1, 0) // (8 * group)
    highest = jnp.minimum(((device + 1) * block_rows + 8 * group) // (8 * group), rows // (8 * group))

    def unpack_group(i, _):
        for j in range(group):
            unpack(i * group + j, 0)
        return 0

    lax.fori_loop(lowest, highest, unpack_group, 0)

    wide_lanes = lax.broadcasted_iota(jnp.int32, (segments, LANES), 1)
    def make_windows(n, stride):
        first_row = device * (block_rows * stride // 8) + 8
        made = {}

        def tile_at(c, row, shift):
            if (c, row, shift) not in made:
                source = (real, imag)[c]
                tile = source[pl.ds(first_row + row, segments, stride=stride), :]
                if shift:
                    after = source[pl.ds(first_row + row + 1, segments, stride=stride), :]
                    tile = jnp.where(wide_lanes >= shift, tile, after).astype(BF16)
                    made[c, row, shift] = pltpu.roll(tile, LANES - shift, 1)
                else:
                    made[c, row, shift] = tile.astype(BF16)
            return made[c, row, shift]

        for o in range(8):
            skip, shift = divmod(16 * stride * o - LANES // 2, LANES)
            for c in range(2):
                for half in range(2):
                    at = (2 * c + half) * LANES
                    windows[n][o * segments : (o + 1) * segments, at : at + LANES] = tile_at(c, skip + half, shift)

    copies = []

    def add_up(t, h):
        total = [None] * 8
        for n, stride in enumerate(strides):
            plane = planes[t // share][n].at[t % share, h]
            if stride < 8:
                starts = [plane[pl.ds(c, LANES // 8, stride=stride), :] for c in range(stride + 1)]
                values = []
                for b in range(8):
                    least = stride * b // 8
                    ahead = phase_ref[n] + stride * b >= 8 * (least + 1)
                    values.append(jnp.where(ahead, starts[least + 1], starts[least]))
                total = values if n == 0 else [x + y for x, y in zip(total, values)]
        for b in range(8):
            acc[(2 * t + h) % 2, pl.ds(b, LANES // 8, stride=8), :] = total[b]
        turned = ((acc[(2 * t + h) % 2] + planes[t // share][len(strides) - 1][t % share, h]) * 0.125).T
        for o in range(4):
            flat[t, pl.ds(4 * h + o, segments, stride=8), :] = turned[o * segments : (o + 1) * segments, :]
        if h:
            copies.append(pltpu.make_async_copy(flat.at[t], out_hbm.at[:, t, :], out_sem.at[t]))
            copies[-1].start()

    phase_copy.wait()
    for g in range(groups):
        own = weights[2 * g * share * LANES : 2 * (g + 1) * share * LANES, :]
        own = own.reshape(2 * share, LANES, 4 * LANES)
        for n, stride in enumerate(strides):
            if g == 0:
                make_windows(n, stride)
            height = 16 * stride
            lhs = own[:, :height].reshape(2 * share * height, 4 * LANES)
            if stride < 8:
                low = 16 * (groups * n + g)
                lhs = jnp.concatenate([lhs, extra[low : low + 16, :]])
            amps = lax.dot_general(
                lhs, windows[n][...], (((1,), (1,)), ((), ())), preferred_element_type=F32
            )
            for t in range(share):
                top = 2 * t * height
                plane = amps[top : top + height] ** 2 + amps[top + height : top + 2 * height] ** 2
                for h in range(2):
                    planes[g][n][t, h, :height] = plane[:, h * 4 * segments : (h + 1) * 4 * segments]
            if stride < 8:
                top = 2 * share * height
                last = amps[top : top + 8] ** 2 + amps[top + 8 : top + 16] ** 2
                for t in range(share):
                    for h in range(2):
                        planes[g][n][t, h, height : height + 1] = last[
                            t : t + 1, h * 4 * segments : (h + 1) * 4 * segments
                        ]
            if g:
                units = range(2 * share * n // len(strides), 2 * share * (n + 1) // len(strides))
                for unit in units:
                    add_up((g - 1) * share + unit // 2, unit % 2)
    for unit in range(2 * share):
        add_up((groups - 1) * share + unit // 2, unit % 2)
    for copy in copies:
        copy.wait()


def search(pieces, layout, weights, extra, base, twist, phases, blocks, templates):
    block_rows = pieces[0].shape[0]
    rows = block_rows * blocks
    strides = STRIDE_TABLE + (8,)
    segments = block_rows // 8
    heights = [min(LANES, 16 * stride + 8) for stride in strides]
    vmem = pl.BlockSpec(memory_space=pltpu.VMEM)
    scratch = [
        ((2 * rows + 16, LANES), F32),
        ((rows + 16, LANES), F32),
        ((rows + 16, LANES), F32),
        ((2, LANES, 4 * segments), F32),
        ((templates, block_rows, LANES), F32),
    ] + len(strides) * [((block_rows, 4 * LANES), BF16)] + GROUPS * [((templates // GROUPS, 2, height, block_rows // 2), F32) for height in heights]
    used = sum(math.prod(shape) * jnp.dtype(kind).itemsize for shape, kind in scratch)
    return pl.pallas_call(
        functools.partial(search_kernel, strides, (block_rows, blocks, templates, layout)),
        out_shape=jax.ShapeDtypeStruct((block_rows, templates, LANES), F32),
        in_specs=[pl.BlockSpec(memory_space=pl.ANY)] + [vmem] * (4 + len(pieces)),
        out_specs=pl.BlockSpec(memory_space=pltpu.HBM),
        scratch_shapes=[
            *[pltpu.VMEM(shape, kind) for shape, kind in scratch[:5]],
            pltpu.SMEM(phases.shape, jnp.int32),
            pltpu.SemaphoreType.DMA((templates,)),
            *[pltpu.VMEM(shape, kind) for shape, kind in scratch[5:]],
        ],
        compiler_params=pltpu.CompilerParams(vmem_limit_bytes=used + 12 * 2**20),
        name="search",
    )(
        phases,
        base,
        twist,
        *pieces,
        weights,
        extra,
    )


def from_across(value, pair):
    blocks, peers = lax.axis_size("bins"), lax.axis_size("fdot")
    pairs = [
        (peers * d + f, peers * (d ^ (pair + 1 - (f ^ (f >> 1)) % 2)) + f)
        for d in range(blocks)
        for f in range(peers)
    ]
    return lax.ppermute(value, ("bins", "fdot"), pairs)


def body(spectrum, bank, fdot_index, harm_map):
    block_len = spectrum.shape[1]
    block_rows = block_len // LANES
    blocks = lax.axis_size("bins")
    templates = fdot_index.shape[0]
    part = lax.axis_index("fdot") & 1
    packed = spectrum.reshape(2, block_rows, LANES).transpose(1, 0, 2).reshape(2 * block_rows, LANES)
    mine = lax.dynamic_slice(packed, (part * block_rows, jnp.int32(0)), (block_rows, LANES))
    far = [from_across(mine, pair) for pair in range(2, blocks, 2)]
    fdot_index, phases = lax.optimization_barrier((fdot_index, harm_map[:, 0, 3]))
    weights, extra, base, twist = template_rows(bank, fdot_index, block_rows * blocks)
    sent, base = lax.optimization_barrier((mine, base))
    held = [sent, from_partner(sent, "bins", 1)]
    layout = [(0, 0), (1, 0)]
    for value, pair in zip(far, range(2, blocks, 2)):
        value = lax.optimization_barrier((value, base))[0]
        held += [value, from_partner(value, "fdot", 2)]
        layout += [(pair, 1), (pair, 0)]
    passed = [from_partner(value, "fdot", 1) for value in held]
    out = search(held + passed, layout, weights, extra, base, twist, phases, blocks, templates)
    return out.transpose(1, 0, 2).reshape(templates, block_len)


def solution(mesh):
    placed = (P(None, ("groups", "bins")), P(), P("fdot"), P(None, "bins", None))
    return jax.shard_map(
        body, mesh=mesh, in_specs=placed, out_specs=P("fdot", ("groups", "bins")), check_vma=False
    )
```

```python
import functools
import math

import jax
import jax.numpy as jnp
from jax import lax
from jax.experimental import pallas as pl
from jax.experimental.pallas import tpu as pltpu
from jax.sharding import PartitionSpec as P

LANES = 128
STRIDE_TABLE = (4, 2, 6, 1, 3, 5, 7)
F32 = jnp.float32
BF16 = jnp.bfloat16
GROUPS = 2


def from_partner(value, axis, mask):
    pairs = [(source, source ^ mask) for source in range(lax.axis_size(axis))]
    return lax.ppermute(value, axis, pairs)


def template_kernel(
    step, groups, index_hbm, phase_hbm, bank_hbm, out_ref, extra_ref, base_ref, twist_ref, wide_ref, index_ref, phase_ref, bank_ref, sem
):
    pairs = ((index_hbm, index_ref), (bank_hbm, bank_ref), (phase_hbm, phase_ref))
    copies = [pltpu.make_async_copy(source, to, sem.at[i]) for i, (source, to) in enumerate(pairs)]
    for copy in copies:
        copy.start()

    row_ids = lax.broadcasted_iota(jnp.int32, (8, LANES), 0)
    lanes = lax.broadcasted_iota(jnp.int32, (8, LANES), 1)
    fine = (row_ids * LANES + lanes).astype(F32) * F32(step)
    base_ref[0:8, :] = jnp.cos(fine)
    base_ref[8:16, :] = jnp.sin(fine)
    chunks = twist_ref.shape[1]
    coarse = lax.broadcasted_iota(jnp.int32, (chunks, LANES), 0).astype(F32)
    coarse = coarse * F32(step * 8 * LANES)
    twist_ref[0] = jnp.cos(coarse)
    twist_ref[1] = jnp.sin(coarse)

    copies[0].wait()
    copies[1].wait()
    zeros = jnp.zeros((1, LANES), F32)

    def banded(row):
        wide = jnp.broadcast_to(jnp.concatenate([row, zeros], axis=1), (LANES, 2 * LANES))
        return pltpu.roll(wide, 0, 1, stride=1, stride_axis=0)

    tables = []
    for t in range(index_ref.shape[0]):
        taps = bank_ref[index_ref[t]].astype(F32)
        real = banded(taps[0:1])
        imag = banded(taps[1:2])
        top, low = 2 * t * LANES, (2 * t + 1) * LANES
        out_ref[top : top + LANES, : 2 * LANES] = real.astype(BF16)
        out_ref[top : top + LANES, 2 * LANES :] = (-imag).astype(BF16)
        out_ref[low : low + LANES, : 2 * LANES] = imag.astype(BF16)
        out_ref[low : low + LANES, 2 * LANES :] = real.astype(BF16)
        tables.append((real, imag))

    count = len(tables)
    for n, stride in enumerate(STRIDE_TABLE):
        at = slice(16 * stride, 16 * stride + 1)
        for g in range(groups):
            some = tables[g * count // groups : (g + 1) * count // groups]
            pad = [jnp.zeros((8 - len(some), 2 * LANES), F32)] if len(some) < 8 else []
            real = jnp.concatenate([value[0][at] for value in some] + pad)
            imag = jnp.concatenate([value[1][at] for value in some] + pad)
            low = 16 * (groups * n + g)
            extra_ref[low : low + 16, : 2 * LANES] = jnp.concatenate([real, imag]).astype(BF16)
            extra_ref[low : low + 16, 2 * LANES :] = jnp.concatenate([-imag, real]).astype(BF16)

    copies[2].wait()
    for n in range(phase_ref.shape[0]):
        wide_ref[16 * n : 16 * n + 16, :] = jnp.full((16, LANES), phase_ref[n], jnp.int32)


def template_rows(bank, fdot_index, phases, rows):
    count = fdot_index.shape[0]
    taps = bank.shape[2]
    height = 2 * count * taps
    vmem = pl.BlockSpec(memory_space=pltpu.VMEM)
    return pl.pallas_call(
        functools.partial(template_kernel, math.pi / (rows * LANES), GROUPS),
        in_specs=[pl.BlockSpec(memory_space=pltpu.HBM)] * 3,
        out_specs=[vmem] * 5,
        out_shape=[
            jax.ShapeDtypeStruct((height, 4 * taps), BF16),
            jax.ShapeDtypeStruct((16 * GROUPS * len(STRIDE_TABLE), 4 * taps), BF16),
            jax.ShapeDtypeStruct((16, LANES), F32),
            jax.ShapeDtypeStruct((2, rows // 8, LANES), F32),
            jax.ShapeDtypeStruct((16 * phases.shape[0], LANES), jnp.int32),
        ],
        scratch_shapes=[
            pltpu.SMEM(fdot_index.shape, jnp.int32),
            pltpu.SMEM(phases.shape, jnp.int32),
            pltpu.VMEM(bank.shape, BF16),
            pltpu.SemaphoreType.DMA((3,)),
        ],
        cost_estimate=pl.CostEstimate(
            flops=4 * height * taps, bytes_accessed=8 * height * taps, transcendentals=0
        ),
        compiler_params=pltpu.CompilerParams(vmem_limit_bytes=16 * 2**20),
        name="template_rows",
    )(fdot_index, phases, bank)


def search_kernel(strides, sizes, phase_ref, base_ref, twist_ref, *refs):
    block_rows, blocks, templates, layout = sizes
    pieces = refs[: 2 * len(layout)]
    weights, extra, out_hbm, raw, real, imag, acc, flat, out_sem, *more = refs[2 * len(layout) :]
    windows = more[: len(strides)]
    more = more[len(strides) :]
    groups = GROUPS
    share = templates // groups
    planes = [more[g * len(strides) : (g + 1) * len(strides)] for g in range(groups)]
    rows = block_rows * blocks
    total_bins = rows * LANES
    segments = block_rows // 8
    device = lax.axis_index("bins")
    peer = lax.axis_index("fdot")
    part = peer & 1
    column = (peer ^ (peer >> 1)) & 1

    sums = [jnp.zeros((8, LANES), F32)] * 4
    for i, source in enumerate(pieces):
        pair, cross = layout[i % len(layout)]
        mask = pair + (column if cross == (i >= len(layout)) else 1 - column) if pair > 1 else pair
        half = part if i < len(layout) else 1 - part
        start = pl.multiple_of((device ^ mask) * (2 * block_rows) + half * block_rows, block_rows)
        for j in range(block_rows // 8):
            tile = source[8 * j : 8 * j + 8, :]
            raw[pl.ds(start + 8 * j, 8), :] = tile
            if j:
                sums[j % 4] = sums[j % 4] + tile * tile
    raw[2 * rows : 2 * rows + 16, :] = raw[0:16, :]
    row_ids = lax.broadcasted_iota(jnp.int32, (8, LANES), 0)
    lanes = lax.broadcasted_iota(jnp.int32, (8, LANES), 1)
    zero_tile = jnp.zeros((8, LANES), F32)
    half_scale = zero_tile + 0.001
    first_tile = raw[0:8, :]
    at_zero = (row_ids < 2) & (lanes == 0)
    zero_bin = jnp.sum(jnp.where(at_zero, first_tile, 0.0), keepdims=True)
    first_tile = jnp.where(at_zero, 0.0, first_tile)
    sums[0] = sums[0] + first_tile * first_tile
    for j in range(1, 2 * blocks):
        tile = raw[j * block_rows : j * block_rows + 8, :]
        sums[j % 4] = sums[j % 4] + tile * tile
    power = jnp.sum((sums[0] + sums[1]) + (sums[2] + sums[3]), keepdims=True)
    mean = jnp.broadcast_to((power + zero_bin * zero_bin) * (1.0 / total_bins) + 1e-06, (8, LANES))
    scale = lax.rsqrt(mean)
    scale = scale * (1.5 - 0.5 * mean * scale * scale)
    half_scale = 0.5 * scale

    base_cos = base_ref[0:8, :]
    base_sin = base_ref[8:16, :]
    mirror_lane = (LANES - lanes) & (LANES - 1)
    mirror_row = 7 - row_ids
    real[0:8, :] = zero_tile
    imag[0:8, :] = zero_tile
    real[rows + 8 : rows + 16, :] = zero_tile
    imag[rows + 8 : rows + 16, :] = zero_tile

    def mirrored(start):
        near = raw[pl.ds(start + 2, 8, stride=2), :]
        far = raw[pl.ds(start, 8, stride=2), :]
        tile = jnp.where(lanes == 0, near, far)
        tile = jnp.take_along_axis(tile, mirror_lane, axis=1, mode="promise_in_bounds")
        return jnp.take_along_axis(tile, mirror_row, axis=0, mode="promise_in_bounds")

    def unpack(chunk, _):
        start = chunk * 16
        a0 = raw[pl.ds(start, 8, stride=2), :]
        a1 = raw[pl.ds(start + 1, 8, stride=2), :]
        back = 2 * rows - 16 - start
        b0 = mirrored(back)
        b1 = mirrored(back + 1)
        chunk_cos = twist_ref[0, pl.ds(chunk, 1), :]
        chunk_sin = twist_ref[1, pl.ds(chunk, 1), :]
        cosine = base_cos * chunk_cos - base_sin * chunk_sin
        sine = base_sin * chunk_cos + base_cos * chunk_sin
        odd_real = a1 + b1
        odd_imag = b0 - a0
        out_real = (a0 + b0) + cosine * odd_real + sine * odd_imag
        out_imag = (a1 - b1) + cosine * odd_imag - sine * odd_real
        place = pl.ds(pl.multiple_of(chunk * 8 + 8, 8), 8)
        real[place, :] = out_real * half_scale
        imag[place, :] = out_imag * half_scale
        return 0

    group = 32
    lowest = jnp.maximum(device * (block_rows // 8) - 1, 0) // (8 * group)
    highest = jnp.minimum(((device + 1) * block_rows + 8 * group) // (8 * group), rows // (8 * group))

    def unpack_group(i, _):
        for j in range(group):
            unpack(i * group + j, 0)
        return 0

    lax.fori_loop(lowest, highest, unpack_group, 0)

    wide_lanes = lax.broadcasted_iota(jnp.int32, (segments, LANES), 1)
    def make_windows(n, stride):
        first_row = device * (block_rows * stride // 8) + 8
        made = {}

        def tile_at(c, row, shift):
            if (c, row, shift) not in made:
                source = (real, imag)[c]
                tile = source[pl.ds(first_row + row, segments, stride=stride), :]
                if shift:
                    after = source[pl.ds(first_row + row + 1, segments, stride=stride), :]
                    tile = jnp.where(wide_lanes >= shift, tile, after).astype(BF16)
                    made[c, row, shift] = pltpu.roll(tile, LANES - shift, 1)
                else:
                    made[c, row, shift] = tile.astype(BF16)
            return made[c, row, shift]

        for o in range(8):
            skip, shift = divmod(16 * stride * o - LANES // 2, LANES)
            for c in range(2):
                for half in range(2):
                    at = (2 * c + half) * LANES
                    windows[n][o * segments : (o + 1) * segments, at : at + LANES] = tile_at(c, skip + half, shift)

    copies = []

    def add_up(t, h):
        total = [None] * 8
        for n, stride in enumerate(strides):
            plane = planes[t // share][n].at[t % share, h]
            if stride < 8:
                starts = [plane[pl.ds(c, LANES // 8, stride=stride), :] for c in range(stride + 1)]
                phase = phase_ref[16 * n : 16 * n + 16, :]
                ahead = {over: phase >= 8 - over for over in {stride * b % 8 for b in range(8)} if over}
                values = []
                for b in range(8):
                    least, over = divmod(stride * b, 8)
                    value = starts[least]
                    values.append(jnp.where(ahead[over], starts[least + 1], value) if over else value)
                total = values if n == 0 else [x + y for x, y in zip(total, values)]
        for b in range(8):
            acc[(2 * t + h) % 2, pl.ds(b, LANES // 8, stride=8), :] = total[b]
        turned = ((acc[(2 * t + h) % 2] + planes[t // share][len(strides) - 1][t % share, h]) * 0.125).T
        for o in range(4):
            flat[t, pl.ds(4 * h + o, segments, stride=8), :] = turned[o * segments : (o + 1) * segments, :]
        if h:
            copies.append(pltpu.make_async_copy(flat.at[t], out_hbm.at[:, t, :], out_sem.at[t]))
            copies[-1].start()

    for g in range(groups):
        own = weights[2 * g * share * LANES : 2 * (g + 1) * share * LANES, :]
        own = own.reshape(2 * share, LANES, 4 * LANES)
        for n, stride in enumerate(strides):
            if g == 0:
                make_windows(n, stride)
            height = 16 * stride
            lhs = own[:, :height].reshape(2 * share * height, 4 * LANES)
            if stride < 8:
                low = 16 * (groups * n + g)
                lhs = jnp.concatenate([lhs, extra[low : low + 16, :]])
            amps = lax.dot_general(
                lhs, windows[n][...], (((1,), (1,)), ((), ())), preferred_element_type=F32
            )
            for t in range(share):
                top = 2 * t * height
                plane = amps[top : top + height] ** 2 + amps[top + height : top + 2 * height] ** 2
                for h in range(2):
                    planes[g][n][t, h, :height] = plane[:, h * 4 * segments : (h + 1) * 4 * segments]
            if stride < 8:
                top = 2 * share * height
                last = amps[top : top + 8] ** 2 + amps[top + 8 : top + 16] ** 2
                for t in range(share):
                    for h in range(2):
                        planes[g][n][t, h, height : height + 1] = last[
                            t : t + 1, h * 4 * segments : (h + 1) * 4 * segments
                        ]
            if g:
                units = range(2 * share * n // len(strides), 2 * share * (n + 1) // len(strides))
                for unit in units:
                    add_up((g - 1) * share + unit // 2, unit % 2)
    for unit in range(2 * share):
        add_up((groups - 1) * share + unit // 2, unit % 2)
    for copy in copies:
        copy.wait()


def search(pieces, layout, weights, extra, base, twist, phases, blocks, templates):
    block_rows = pieces[0].shape[0]
    rows = block_rows * blocks
    strides = STRIDE_TABLE + (8,)
    segments = block_rows // 8
    heights = [min(LANES, 16 * stride + 8) for stride in strides]
    vmem = pl.BlockSpec(memory_space=pltpu.VMEM)
    scratch = [
        ((2 * rows + 16, LANES), F32),
        ((rows + 16, LANES), F32),
        ((rows + 16, LANES), F32),
        ((2, LANES, 4 * segments), F32),
        ((templates, block_rows, LANES), F32),
    ] + len(strides) * [((block_rows, 4 * LANES), BF16)] + GROUPS * [((templates // GROUPS, 2, height, block_rows // 2), F32) for height in heights]
    used = sum(math.prod(shape) * jnp.dtype(kind).itemsize for shape, kind in scratch)
    return pl.pallas_call(
        functools.partial(search_kernel, strides, (block_rows, blocks, templates, layout)),
        out_shape=jax.ShapeDtypeStruct((block_rows, templates, LANES), F32),
        in_specs=[vmem] * (5 + len(pieces)),
        out_specs=pl.BlockSpec(memory_space=pltpu.HBM),
        scratch_shapes=[
            *[pltpu.VMEM(shape, kind) for shape, kind in scratch[:5]],
            pltpu.SemaphoreType.DMA((templates,)),
            *[pltpu.VMEM(shape, kind) for shape, kind in scratch[5:]],
        ],
        compiler_params=pltpu.CompilerParams(vmem_limit_bytes=used + 12 * 2**20),
        name="search",
    )(
        phases,
        base,
        twist,
        *pieces,
        weights,
        extra,
    )


def from_across(value, pair):
    blocks, peers = lax.axis_size("bins"), lax.axis_size("fdot")
    pairs = [
        (peers * d + f, peers * (d ^ (pair + 1 - (f ^ (f >> 1)) % 2)) + f)
        for d in range(blocks)
        for f in range(peers)
    ]
    return lax.ppermute(value, ("bins", "fdot"), pairs)


def body(spectrum, bank, fdot_index, harm_map):
    block_len = spectrum.shape[1]
    block_rows = block_len // LANES
    blocks = lax.axis_size("bins")
    templates = fdot_index.shape[0]
    part = lax.axis_index("fdot") & 1
    packed = spectrum.reshape(2, block_rows, LANES).transpose(1, 0, 2).reshape(2 * block_rows, LANES)
    mine = lax.dynamic_slice(packed, (part * block_rows, jnp.int32(0)), (block_rows, LANES))
    far = [from_across(mine, pair) for pair in range(2, blocks, 2)]
    fdot_index, phases = lax.optimization_barrier((fdot_index, harm_map[:, 0, 3]))
    weights, extra, base, twist, phases = template_rows(bank, fdot_index, phases, block_rows * blocks)
    sent, base = lax.optimization_barrier((mine, base))
    held = [sent, from_partner(sent, "bins", 1)]
    layout = [(0, 0), (1, 0)]
    for value, pair in zip(far, range(2, blocks, 2)):
        value = lax.optimization_barrier((value, base))[0]
        held += [value, from_partner(value, "fdot", 2)]
        layout += [(pair, 1), (pair, 0)]
    passed = [from_partner(value, "fdot", 1) for value in held]
    out = search(held + passed, layout, weights, extra, base, twist, phases, blocks, templates)
    return out.transpose(1, 0, 2).reshape(templates, block_len)


def solution(mesh):
    placed = (P(None, ("groups", "bins")), P(), P("fdot"), P(None, "bins", None))
    return jax.shard_map(
        body, mesh=mesh, in_specs=placed, out_specs=P("fdot", ("groups", "bins")), check_vma=False
    )
```

```python
import functools
import math

import jax
import jax.numpy as jnp
from jax import lax
from jax.experimental import pallas as pl
from jax.experimental.pallas import tpu as pltpu
from jax.sharding import PartitionSpec as P

LANES = 128
STRIDE_TABLE = (4, 2, 6, 1, 3, 5, 7)
F32 = jnp.float32
BF16 = jnp.bfloat16
GROUPS = 1


def from_partner(value, axis, mask):
    pairs = [(source, source ^ mask) for source in range(lax.axis_size(axis))]
    return lax.ppermute(value, axis, pairs)


def template_kernel(
    step, groups, index_hbm, phase_hbm, bank_hbm, out_ref, extra_ref, base_ref, twist_ref, wide_ref, index_ref, phase_ref, bank_ref, sem
):
    pairs = ((index_hbm, index_ref), (bank_hbm, bank_ref), (phase_hbm, phase_ref))
    copies = [pltpu.make_async_copy(source, to, sem.at[i]) for i, (source, to) in enumerate(pairs)]
    for copy in copies:
        copy.start()

    row_ids = lax.broadcasted_iota(jnp.int32, (8, LANES), 0)
    lanes = lax.broadcasted_iota(jnp.int32, (8, LANES), 1)
    fine = (row_ids * LANES + lanes).astype(F32) * F32(step)
    base_ref[0:8, :] = jnp.cos(fine)
    base_ref[8:16, :] = jnp.sin(fine)
    chunks = twist_ref.shape[1]
    coarse = lax.broadcasted_iota(jnp.int32, (chunks, LANES), 0).astype(F32)
    coarse = coarse * F32(step * 8 * LANES)
    twist_ref[0] = jnp.cos(coarse)
    twist_ref[1] = jnp.sin(coarse)

    copies[0].wait()
    copies[1].wait()
    zeros = jnp.zeros((1, LANES), F32)

    def banded(row):
        wide = jnp.broadcast_to(jnp.concatenate([row, zeros], axis=1), (LANES, 2 * LANES))
        return pltpu.roll(wide, 0, 1, stride=1, stride_axis=0)

    tables = []
    for t in range(index_ref.shape[0]):
        taps = bank_ref[index_ref[t]].astype(F32)
        real = banded(taps[0:1])
        imag = banded(taps[1:2])
        top, low = 2 * t * LANES, (2 * t + 1) * LANES
        out_ref[top : top + LANES, : 2 * LANES] = real.astype(BF16)
        out_ref[top : top + LANES, 2 * LANES :] = (-imag).astype(BF16)
        out_ref[low : low + LANES, : 2 * LANES] = imag.astype(BF16)
        out_ref[low : low + LANES, 2 * LANES :] = real.astype(BF16)
        tables.append((real, imag))

    count = len(tables)
    for n, stride in enumerate(STRIDE_TABLE):
        at = slice(16 * stride, 16 * stride + 1)
        for g in range(groups):
            some = tables[g * count // groups : (g + 1) * count // groups]
            pad = [jnp.zeros((8 - len(some), 2 * LANES), F32)] if len(some) < 8 else []
            real = jnp.concatenate([value[0][at] for value in some] + pad)
            imag = jnp.concatenate([value[1][at] for value in some] + pad)
            low = 16 * (groups * n + g)
            extra_ref[low : low + 16, : 2 * LANES] = jnp.concatenate([real, imag]).astype(BF16)
            extra_ref[low : low + 16, 2 * LANES :] = jnp.concatenate([-imag, real]).astype(BF16)

    copies[2].wait()
    for n in range(phase_ref.shape[0]):
        wide_ref[16 * n : 16 * n + 16, :] = jnp.full((16, LANES), phase_ref[n], jnp.int32)


def template_rows(bank, fdot_index, phases, rows):
    count = fdot_index.shape[0]
    taps = bank.shape[2]
    height = 2 * count * taps
    vmem = pl.BlockSpec(memory_space=pltpu.VMEM)
    return pl.pallas_call(
        functools.partial(template_kernel, math.pi / (rows * LANES), GROUPS),
        in_specs=[pl.BlockSpec(memory_space=pltpu.HBM)] * 3,
        out_specs=[vmem] * 5,
        out_shape=[
            jax.ShapeDtypeStruct((height, 4 * taps), BF16),
            jax.ShapeDtypeStruct((16 * GROUPS * len(STRIDE_TABLE), 4 * taps), BF16),
            jax.ShapeDtypeStruct((16, LANES), F32),
            jax.ShapeDtypeStruct((2, rows // 8, LANES), F32),
            jax.ShapeDtypeStruct((16 * phases.shape[0], LANES), jnp.int32),
        ],
        scratch_shapes=[
            pltpu.SMEM(fdot_index.shape, jnp.int32),
            pltpu.SMEM(phases.shape, jnp.int32),
            pltpu.VMEM(bank.shape, BF16),
            pltpu.SemaphoreType.DMA((3,)),
        ],
        cost_estimate=pl.CostEstimate(
            flops=4 * height * taps, bytes_accessed=8 * height * taps, transcendentals=0
        ),
        compiler_params=pltpu.CompilerParams(vmem_limit_bytes=16 * 2**20),
        name="template_rows",
    )(fdot_index, phases, bank)


def search_kernel(strides, sizes, phase_ref, base_ref, twist_ref, *refs):
    block_rows, blocks, templates, layout = sizes
    pieces = refs[: 2 * len(layout)]
    weights, extra, out_hbm, raw, real, imag, acc, flat, out_sem, *more = refs[2 * len(layout) :]
    windows = more[: len(strides)]
    more = more[len(strides) :]
    groups = GROUPS
    share = templates // groups
    planes = [more[g * len(strides) : (g + 1) * len(strides)] for g in range(groups)]
    rows = block_rows * blocks
    total_bins = rows * LANES
    segments = block_rows // 8
    device = lax.axis_index("bins")
    peer = lax.axis_index("fdot")
    part = peer & 1
    column = (peer ^ (peer >> 1)) & 1

    sums = [jnp.zeros((8, LANES), F32)] * 4
    for i, source in enumerate(pieces):
        pair, cross = layout[i % len(layout)]
        mask = pair + (column if cross == (i >= len(layout)) else 1 - column) if pair > 1 else pair
        half = part if i < len(layout) else 1 - part
        start = pl.multiple_of((device ^ mask) * (2 * block_rows) + half * block_rows, block_rows)
        for j in range(block_rows // 8):
            tile = source[8 * j : 8 * j + 8, :]
            raw[pl.ds(start + 8 * j, 8), :] = tile
            if j:
                sums[j % 4] = sums[j % 4] + tile * tile
    raw[2 * rows : 2 * rows + 16, :] = raw[0:16, :]
    row_ids = lax.broadcasted_iota(jnp.int32, (8, LANES), 0)
    lanes = lax.broadcasted_iota(jnp.int32, (8, LANES), 1)
    zero_tile = jnp.zeros((8, LANES), F32)
    half_scale = zero_tile + 0.001
    first_tile = raw[0:8, :]
    at_zero = (row_ids < 2) & (lanes == 0)
    zero_bin = jnp.sum(jnp.where(at_zero, first_tile, 0.0), keepdims=True)
    first_tile = jnp.where(at_zero, 0.0, first_tile)
    sums[0] = sums[0] + first_tile * first_tile
    for j in range(1, 2 * blocks):
        tile = raw[j * block_rows : j * block_rows + 8, :]
        sums[j % 4] = sums[j % 4] + tile * tile
    power = jnp.sum((sums[0] + sums[1]) + (sums[2] + sums[3]), keepdims=True)
    mean = jnp.broadcast_to((power + zero_bin * zero_bin) * (1.0 / total_bins) + 1e-06, (8, LANES))
    scale = lax.rsqrt(mean)
    scale = scale * (1.5 - 0.5 * mean * scale * scale)
    half_scale = 0.5 * scale

    base_cos = base_ref[0:8, :]
    base_sin = base_ref[8:16, :]
    mirror_lane = (LANES - lanes) & (LANES - 1)
    mirror_row = 7 - row_ids
    real[0:8, :] = zero_tile
    imag[0:8, :] = zero_tile
    real[rows + 8 : rows + 16, :] = zero_tile
    imag[rows + 8 : rows + 16, :] = zero_tile

    def mirrored(start):
        near = raw[pl.ds(start + 2, 8, stride=2), :]
        far = raw[pl.ds(start, 8, stride=2), :]
        tile = jnp.where(lanes == 0, near, far)
        tile = jnp.take_along_axis(tile, mirror_lane, axis=1, mode="promise_in_bounds")
        return jnp.take_along_axis(tile, mirror_row, axis=0, mode="promise_in_bounds")

    def unpack(chunk, _):
        start = chunk * 16
        a0 = raw[pl.ds(start, 8, stride=2), :]
        a1 = raw[pl.ds(start + 1, 8, stride=2), :]
        back = 2 * rows - 16 - start
        b0 = mirrored(back)
        b1 = mirrored(back + 1)
        chunk_cos = twist_ref[0, pl.ds(chunk, 1), :]
        chunk_sin = twist_ref[1, pl.ds(chunk, 1), :]
        cosine = base_cos * chunk_cos - base_sin * chunk_sin
        sine = base_sin * chunk_cos + base_cos * chunk_sin
        odd_real = a1 + b1
        odd_imag = b0 - a0
        out_real = (a0 + b0) + cosine * odd_real + sine * odd_imag
        out_imag = (a1 - b1) + cosine * odd_imag - sine * odd_real
        place = pl.ds(pl.multiple_of(chunk * 8 + 8, 8), 8)
        real[place, :] = out_real * half_scale
        imag[place, :] = out_imag * half_scale
        return 0

    group = 32
    lowest = jnp.maximum(device * (block_rows // 8) - 1, 0) // (8 * group)
    highest = jnp.minimum(((device + 1) * block_rows + 8 * group) // (8 * group), rows // (8 * group))

    def unpack_group(i, _):
        for j in range(group):
            unpack(i * group + j, 0)
        return 0

    lax.fori_loop(lowest, highest, unpack_group, 0)

    wide_lanes = lax.broadcasted_iota(jnp.int32, (segments, LANES), 1)
    def make_windows(n, stride):
        first_row = device * (block_rows * stride // 8) + 8
        made = {}

        def tile_at(c, row, shift):
            if (c, row, shift) not in made:
                source = (real, imag)[c]
                tile = source[pl.ds(first_row + row, segments, stride=stride), :]
                if shift:
                    after = source[pl.ds(first_row + row + 1, segments, stride=stride), :]
                    tile = jnp.where(wide_lanes >= shift, tile, after).astype(BF16)
                    made[c, row, shift] = pltpu.roll(tile, LANES - shift, 1)
                else:
                    made[c, row, shift] = tile.astype(BF16)
            return made[c, row, shift]

        for o in range(8):
            skip, shift = divmod(16 * stride * o - LANES // 2, LANES)
            for c in range(2):
                for half in range(2):
                    at = (2 * c + half) * LANES
                    windows[n][o * segments : (o + 1) * segments, at : at + LANES] = tile_at(c, skip + half, shift)

    copies = []

    def add_up(t, h):
        total = [None] * 8
        for n, stride in enumerate(strides):
            plane = planes[t // share][n].at[t % share, h]
            if stride < 8:
                starts = [plane[pl.ds(c, LANES // 8, stride=stride), :] for c in range(stride + 1)]
                phase = phase_ref[16 * n : 16 * n + 16, :]
                ahead = {over: phase >= 8 - over for over in {stride * b % 8 for b in range(8)} if over}
                values = []
                for b in range(8):
                    least, over = divmod(stride * b, 8)
                    value = starts[least]
                    values.append(jnp.where(ahead[over], starts[least + 1], value) if over else value)
                total = values if n == 0 else [x + y for x, y in zip(total, values)]
        for b in range(8):
            acc[(2 * t + h) % 2, pl.ds(b, LANES // 8, stride=8), :] = total[b]
        turned = ((acc[(2 * t + h) % 2] + planes[t // share][len(strides) - 1][t % share, h]) * 0.125).T
        for o in range(4):
            flat[t, pl.ds(4 * h + o, segments, stride=8), :] = turned[o * segments : (o + 1) * segments, :]
        if h:
            copies.append(pltpu.make_async_copy(flat.at[t], out_hbm.at[:, t, :], out_sem.at[t]))
            copies[-1].start()

    for g in range(groups):
        own = weights[2 * g * share * LANES : 2 * (g + 1) * share * LANES, :]
        own = own.reshape(2 * share, LANES, 4 * LANES)
        for n, stride in enumerate(strides):
            if g == 0:
                make_windows(n, stride)
            height = 16 * stride
            lhs = own[:, :height].reshape(2 * share * height, 4 * LANES)
            if stride < 8:
                low = 16 * (groups * n + g)
                lhs = jnp.concatenate([lhs, extra[low : low + 16, :]])
            amps = lax.dot_general(
                lhs, windows[n][...], (((1,), (1,)), ((), ())), preferred_element_type=F32
            )
            for t in range(share):
                top = 2 * t * height
                plane = amps[top : top + height] ** 2 + amps[top + height : top + 2 * height] ** 2
                for h in range(2):
                    planes[g][n][t, h, :height] = plane[:, h * 4 * segments : (h + 1) * 4 * segments]
            if stride < 8:
                top = 2 * share * height
                last = amps[top : top + 8] ** 2 + amps[top + 8 : top + 16] ** 2
                for t in range(share):
                    for h in range(2):
                        planes[g][n][t, h, height : height + 1] = last[
                            t : t + 1, h * 4 * segments : (h + 1) * 4 * segments
                        ]
            if g:
                units = range(2 * share * n // len(strides), 2 * share * (n + 1) // len(strides))
                for unit in units:
                    add_up((g - 1) * share + unit // 2, unit % 2)
    for unit in range(2 * share):
        add_up((groups - 1) * share + unit // 2, unit % 2)
    for copy in copies:
        copy.wait()


def search(pieces, layout, weights, extra, base, twist, phases, blocks, templates):
    block_rows = pieces[0].shape[0]
    rows = block_rows * blocks
    strides = STRIDE_TABLE + (8,)
    segments = block_rows // 8
    heights = [min(LANES, 16 * stride + 8) for stride in strides]
    vmem = pl.BlockSpec(memory_space=pltpu.VMEM)
    scratch = [
        ((2 * rows + 16, LANES), F32),
        ((rows + 16, LANES), F32),
        ((rows + 16, LANES), F32),
        ((2, LANES, 4 * segments), F32),
        ((templates, block_rows, LANES), F32),
    ] + len(strides) * [((block_rows, 4 * LANES), BF16)] + GROUPS * [((templates // GROUPS, 2, height, block_rows // 2), F32) for height in heights]
    used = sum(math.prod(shape) * jnp.dtype(kind).itemsize for shape, kind in scratch)
    return pl.pallas_call(
        functools.partial(search_kernel, strides, (block_rows, blocks, templates, layout)),
        out_shape=jax.ShapeDtypeStruct((block_rows, templates, LANES), F32),
        in_specs=[vmem] * (5 + len(pieces)),
        out_specs=pl.BlockSpec(memory_space=pltpu.HBM),
        scratch_shapes=[
            *[pltpu.VMEM(shape, kind) for shape, kind in scratch[:5]],
            pltpu.SemaphoreType.DMA((templates,)),
            *[pltpu.VMEM(shape, kind) for shape, kind in scratch[5:]],
        ],
        compiler_params=pltpu.CompilerParams(vmem_limit_bytes=used + 12 * 2**20),
        name="search",
    )(
        phases,
        base,
        twist,
        *pieces,
        weights,
        extra,
    )


def from_across(value, pair):
    blocks, peers = lax.axis_size("bins"), lax.axis_size("fdot")
    pairs = [
        (peers * d + f, peers * (d ^ (pair + 1 - (f ^ (f >> 1)) % 2)) + f)
        for d in range(blocks)
        for f in range(peers)
    ]
    return lax.ppermute(value, ("bins", "fdot"), pairs)


def body(spectrum, bank, fdot_index, harm_map):
    block_len = spectrum.shape[1]
    block_rows = block_len // LANES
    blocks = lax.axis_size("bins")
    templates = fdot_index.shape[0]
    part = lax.axis_index("fdot") & 1
    packed = spectrum.reshape(2, block_rows, LANES).transpose(1, 0, 2).reshape(2 * block_rows, LANES)
    mine = lax.dynamic_slice(packed, (part * block_rows, jnp.int32(0)), (block_rows, LANES))
    far = [from_across(mine, pair) for pair in range(2, blocks, 2)]
    fdot_index, phases = lax.optimization_barrier((fdot_index, harm_map[:, 0, 3]))
    weights, extra, base, twist, phases = template_rows(bank, fdot_index, phases, block_rows * blocks)
    sent, base = lax.optimization_barrier((mine, base))
    held = [sent, from_partner(sent, "bins", 1)]
    layout = [(0, 0), (1, 0)]
    for value, pair in zip(far, range(2, blocks, 2)):
        value = lax.optimization_barrier((value, base))[0]
        held += [value, from_partner(value, "fdot", 2)]
        layout += [(pair, 1), (pair, 0)]
    passed = [from_partner(value, "fdot", 1) for value in held]
    out = search(held + passed, layout, weights, extra, base, twist, phases, blocks, templates)
    return out.transpose(1, 0, 2).reshape(templates, block_len)


def solution(mesh):
    placed = (P(None, ("groups", "bins")), P(), P("fdot"), P(None, "bins", None))
    return jax.shard_map(
        body, mesh=mesh, in_specs=placed, out_specs=P("fdot", ("groups", "bins")), check_vma=False
    )
```

```python
import functools
import math

import jax
import jax.numpy as jnp
from jax import lax
from jax.experimental import pallas as pl
from jax.experimental.pallas import tpu as pltpu
from jax.sharding import PartitionSpec as P

LANES = 128
STRIDE_TABLE = (4, 2, 6, 1, 3, 5, 7)
F32 = jnp.float32
BF16 = jnp.bfloat16
GROUPS = 1


def from_partner(value, axis, mask):
    pairs = [(source, source ^ mask) for source in range(lax.axis_size(axis))]
    return lax.ppermute(value, axis, pairs)


def template_kernel(
    step, groups, index_hbm, phase_hbm, bank_hbm, out_ref, extra_ref, base_ref, twist_ref, wide_ref, index_ref, phase_ref, bank_ref, sem
):
    pairs = ((index_hbm, index_ref), (bank_hbm, bank_ref), (phase_hbm, phase_ref))
    copies = [pltpu.make_async_copy(source, to, sem.at[i]) for i, (source, to) in enumerate(pairs)]
    for copy in copies:
        copy.start()

    row_ids = lax.broadcasted_iota(jnp.int32, (8, LANES), 0)
    lanes = lax.broadcasted_iota(jnp.int32, (8, LANES), 1)
    fine = (row_ids * LANES + lanes).astype(F32) * F32(step)
    base_ref[0:8, :] = jnp.cos(fine)
    base_ref[8:16, :] = jnp.sin(fine)
    chunks = twist_ref.shape[1]
    coarse = lax.broadcasted_iota(jnp.int32, (chunks, LANES), 0).astype(F32)
    coarse = coarse * F32(step * 8 * LANES)
    twist_ref[0] = jnp.cos(coarse)
    twist_ref[1] = jnp.sin(coarse)

    copies[0].wait()
    copies[1].wait()
    zeros = jnp.zeros((1, LANES), F32)

    def banded(row):
        wide = jnp.broadcast_to(jnp.concatenate([row, zeros], axis=1), (LANES, 2 * LANES))
        return pltpu.roll(wide, 0, 1, stride=1, stride_axis=0)

    tables = []
    for t in range(index_ref.shape[0]):
        taps = bank_ref[index_ref[t]].astype(F32)
        real = banded(taps[0:1])
        imag = banded(taps[1:2])
        top, low = 2 * t * LANES, (2 * t + 1) * LANES
        out_ref[top : top + LANES, : 2 * LANES] = real.astype(BF16)
        out_ref[top : top + LANES, 2 * LANES :] = (-imag).astype(BF16)
        out_ref[low : low + LANES, : 2 * LANES] = imag.astype(BF16)
        out_ref[low : low + LANES, 2 * LANES :] = real.astype(BF16)
        tables.append((real, imag))

    count = len(tables)
    for n, stride in enumerate(STRIDE_TABLE):
        at = slice(16 * stride, 16 * stride + 1)
        for g in range(groups):
            some = tables[g * count // groups : (g + 1) * count // groups]
            pad = [jnp.zeros((8 - len(some), 2 * LANES), F32)] if len(some) < 8 else []
            real = jnp.concatenate([value[0][at] for value in some] + pad)
            imag = jnp.concatenate([value[1][at] for value in some] + pad)
            low = 16 * (groups * n + g)
            extra_ref[low : low + 16, : 2 * LANES] = jnp.concatenate([real, imag]).astype(BF16)
            extra_ref[low : low + 16, 2 * LANES :] = jnp.concatenate([-imag, real]).astype(BF16)

    copies[2].wait()
    for n in range(phase_ref.shape[0]):
        wide_ref[16 * n : 16 * n + 16, :] = jnp.full((16, LANES), phase_ref[n], jnp.int32)


def template_rows(bank, fdot_index, phases, rows):
    count = fdot_index.shape[0]
    taps = bank.shape[2]
    height = 2 * count * taps
    vmem = pl.BlockSpec(memory_space=pltpu.VMEM)
    return pl.pallas_call(
        functools.partial(template_kernel, math.pi / (rows * LANES), GROUPS),
        in_specs=[pl.BlockSpec(memory_space=pltpu.HBM)] * 3,
        out_specs=[vmem] * 5,
        out_shape=[
            jax.ShapeDtypeStruct((height, 4 * taps), BF16),
            jax.ShapeDtypeStruct((16 * GROUPS * len(STRIDE_TABLE), 4 * taps), BF16),
            jax.ShapeDtypeStruct((16, LANES), F32),
            jax.ShapeDtypeStruct((2, rows // 8, LANES), F32),
            jax.ShapeDtypeStruct((16 * phases.shape[0], LANES), jnp.int32),
        ],
        scratch_shapes=[
            pltpu.SMEM(fdot_index.shape, jnp.int32),
            pltpu.SMEM(phases.shape, jnp.int32),
            pltpu.VMEM(bank.shape, BF16),
            pltpu.SemaphoreType.DMA((3,)),
        ],
        cost_estimate=pl.CostEstimate(
            flops=4 * height * taps, bytes_accessed=8 * height * taps, transcendentals=0
        ),
        compiler_params=pltpu.CompilerParams(vmem_limit_bytes=16 * 2**20),
        name="template_rows",
    )(fdot_index, phases, bank)


def search_kernel(strides, sizes, phase_ref, base_ref, twist_ref, *refs):
    block_rows, blocks, templates, layout = sizes
    pieces = refs[: 2 * len(layout)]
    weights, extra, out_hbm, raw, real, imag, acc, flat, out_sem, *more = refs[2 * len(layout) :]
    windows = more[: len(strides)]
    more = more[len(strides) :]
    groups = GROUPS
    share = templates // groups
    planes = [more[g * len(strides) : (g + 1) * len(strides)] for g in range(groups)]
    rows = block_rows * blocks
    total_bins = rows * LANES
    segments = block_rows // 8
    device = lax.axis_index("bins")
    peer = lax.axis_index("fdot")
    part = peer & 1
    column = (peer ^ (peer >> 1)) & 1

    sums = [jnp.zeros((8, LANES), F32)] * 4
    for i, source in enumerate(pieces):
        pair, cross = layout[i % len(layout)]
        mask = pair + (column if cross == (i >= len(layout)) else 1 - column) if pair > 1 else pair
        half = part if i < len(layout) else 1 - part
        start = pl.multiple_of((device ^ mask) * (2 * block_rows) + half * block_rows, block_rows)
        for j in range(block_rows // 8):
            tile = source[8 * j : 8 * j + 8, :]
            raw[pl.ds(start + 8 * j, 8), :] = tile
            if j:
                sums[j % 4] = sums[j % 4] + tile * tile
    raw[2 * rows : 2 * rows + 16, :] = raw[0:16, :]
    row_ids = lax.broadcasted_iota(jnp.int32, (8, LANES), 0)
    lanes = lax.broadcasted_iota(jnp.int32, (8, LANES), 1)
    zero_tile = jnp.zeros((8, LANES), F32)
    half_scale = zero_tile + 0.001
    first_tile = raw[0:8, :]
    at_zero = (row_ids < 2) & (lanes == 0)
    zero_bin = jnp.sum(jnp.where(at_zero, first_tile, 0.0), keepdims=True)
    first_tile = jnp.where(at_zero, 0.0, first_tile)
    sums[0] = sums[0] + first_tile * first_tile
    for j in range(1, 2 * blocks):
        tile = raw[j * block_rows : j * block_rows + 8, :]
        sums[j % 4] = sums[j % 4] + tile * tile
    power = jnp.sum((sums[0] + sums[1]) + (sums[2] + sums[3]), keepdims=True)
    mean = jnp.broadcast_to((power + zero_bin * zero_bin) * (1.0 / total_bins) + 1e-06, (8, LANES))
    scale = lax.rsqrt(mean)
    scale = scale * (1.5 - 0.5 * mean * scale * scale)
    half_scale = 0.5 * scale

    base_cos = base_ref[0:8, :]
    base_sin = base_ref[8:16, :]
    mirror_lane = (LANES - lanes) & (LANES - 1)
    mirror_row = 7 - row_ids
    real[0:8, :] = zero_tile
    imag[0:8, :] = zero_tile
    real[rows + 8 : rows + 16, :] = zero_tile
    imag[rows + 8 : rows + 16, :] = zero_tile

    def mirrored(start):
        near = raw[pl.ds(start + 2, 8, stride=2), :]
        far = raw[pl.ds(start, 8, stride=2), :]
        tile = jnp.where(lanes == 0, near, far)
        tile = jnp.take_along_axis(tile, mirror_lane, axis=1, mode="promise_in_bounds")
        return jnp.take_along_axis(tile, mirror_row, axis=0, mode="promise_in_bounds")

    def unpack(chunk, _):
        start = chunk * 16
        a0 = raw[pl.ds(start, 8, stride=2), :]
        a1 = raw[pl.ds(start + 1, 8, stride=2), :]
        back = 2 * rows - 16 - start
        b0 = mirrored(back)
        b1 = mirrored(back + 1)
        chunk_cos = twist_ref[0, pl.ds(chunk, 1), :]
        chunk_sin = twist_ref[1, pl.ds(chunk, 1), :]
        cosine = base_cos * chunk_cos - base_sin * chunk_sin
        sine = base_sin * chunk_cos + base_cos * chunk_sin
        odd_real = a1 + b1
        odd_imag = b0 - a0
        out_real = (a0 + b0) + cosine * odd_real + sine * odd_imag
        out_imag = (a1 - b1) + cosine * odd_imag - sine * odd_real
        place = pl.ds(pl.multiple_of(chunk * 8 + 8, 8), 8)
        real[place, :] = out_real * half_scale
        imag[place, :] = out_imag * half_scale
        return 0

    group = 16
    lowest = jnp.maximum(device * (block_rows // 8) - 1, 0) // (8 * group)
    highest = jnp.minimum(((device + 1) * block_rows + 8 * group) // (8 * group), rows // (8 * group))

    def unpack_group(i, _):
        for j in range(group):
            unpack(i * group + j, 0)
        return 0

    lax.fori_loop(lowest, highest, unpack_group, 0)

    wide_lanes = lax.broadcasted_iota(jnp.int32, (segments, LANES), 1)
    def make_windows(n, stride):
        first_row = device * (block_rows * stride // 8) + 8
        made = {}

        def tile_at(c, row, shift):
            if (c, row, shift) not in made:
                source = (real, imag)[c]
                tile = source[pl.ds(first_row + row, segments, stride=stride), :]
                if shift:
                    after = source[pl.ds(first_row + row + 1, segments, stride=stride), :]
                    tile = jnp.where(wide_lanes >= shift, tile, after).astype(BF16)
                    made[c, row, shift] = pltpu.roll(tile, LANES - shift, 1)
                else:
                    made[c, row, shift] = tile.astype(BF16)
            return made[c, row, shift]

        for o in range(8):
            skip, shift = divmod(16 * stride * o - LANES // 2, LANES)
            for c in range(2):
                for half in range(2):
                    at = (2 * c + half) * LANES
                    windows[n][o * segments : (o + 1) * segments, at : at + LANES] = tile_at(c, skip + half, shift)

    copies = []

    def add_up(t, h):
        total = [None] * 8
        for n, stride in enumerate(strides):
            plane = planes[t // share][n].at[t % share, h]
            if stride < 8:
                starts = [plane[pl.ds(c, LANES // 8, stride=stride), :] for c in range(stride + 1)]
                phase = phase_ref[16 * n : 16 * n + 16, :]
                ahead = {over: phase >= 8 - over for over in {stride * b % 8 for b in range(8)} if over}
                values = []
                for b in range(8):
                    least, over = divmod(stride * b, 8)
                    value = starts[least]
                    values.append(jnp.where(ahead[over], starts[least + 1], value) if over else value)
                total = values if n == 0 else [x + y for x, y in zip(total, values)]
        for b in range(8):
            acc[(2 * t + h) % 2, pl.ds(b, LANES // 8, stride=8), :] = total[b]
        turned = ((acc[(2 * t + h) % 2] + planes[t // share][len(strides) - 1][t % share, h]) * 0.125).T
        for o in range(4):
            flat[t, pl.ds(4 * h + o, segments, stride=8), :] = turned[o * segments : (o + 1) * segments, :]
        if h:
            copies.append(pltpu.make_async_copy(flat.at[t], out_hbm.at[:, t, :], out_sem.at[t]))
            copies[-1].start()

    for g in range(groups):
        own = weights[2 * g * share * LANES : 2 * (g + 1) * share * LANES, :]
        own = own.reshape(2 * share, LANES, 4 * LANES)
        for n, stride in enumerate(strides):
            if g == 0:
                make_windows(n, stride)
            height = 16 * stride
            lhs = own[:, :height].reshape(2 * share * height, 4 * LANES)
            if stride < 8:
                low = 16 * (groups * n + g)
                lhs = jnp.concatenate([lhs, extra[low : low + 16, :]])
            amps = lax.dot_general(
                lhs, windows[n][...], (((1,), (1,)), ((), ())), preferred_element_type=F32
            )
            for t in range(share):
                top = 2 * t * height
                plane = amps[top : top + height] ** 2 + amps[top + height : top + 2 * height] ** 2
                for h in range(2):
                    planes[g][n][t, h, :height] = plane[:, h * 4 * segments : (h + 1) * 4 * segments]
            if stride < 8:
                top = 2 * share * height
                last = amps[top : top + 8] ** 2 + amps[top + 8 : top + 16] ** 2
                for t in range(share):
                    for h in range(2):
                        planes[g][n][t, h, height : height + 1] = last[
                            t : t + 1, h * 4 * segments : (h + 1) * 4 * segments
                        ]
            if g:
                units = range(2 * share * n // len(strides), 2 * share * (n + 1) // len(strides))
                for unit in units:
                    add_up((g - 1) * share + unit // 2, unit % 2)
    for unit in range(2 * share):
        add_up((groups - 1) * share + unit // 2, unit % 2)
    for copy in copies:
        copy.wait()


def search(pieces, layout, weights, extra, base, twist, phases, blocks, templates):
    block_rows = pieces[0].shape[0]
    rows = block_rows * blocks
    strides = STRIDE_TABLE + (8,)
    segments = block_rows // 8
    heights = [min(LANES, 16 * stride + 8) for stride in strides]
    vmem = pl.BlockSpec(memory_space=pltpu.VMEM)
    scratch = [
        ((2 * rows + 16, LANES), F32),
        ((rows + 16, LANES), F32),
        ((rows + 16, LANES), F32),
        ((2, LANES, 4 * segments), F32),
        ((templates, block_rows, LANES), F32),
    ] + len(strides) * [((block_rows, 4 * LANES), BF16)] + GROUPS * [((templates // GROUPS, 2, height, block_rows // 2), F32) for height in heights]
    used = sum(math.prod(shape) * jnp.dtype(kind).itemsize for shape, kind in scratch)
    return pl.pallas_call(
        functools.partial(search_kernel, strides, (block_rows, blocks, templates, layout)),
        out_shape=jax.ShapeDtypeStruct((block_rows, templates, LANES), F32),
        in_specs=[vmem] * (5 + len(pieces)),
        out_specs=pl.BlockSpec(memory_space=pltpu.HBM),
        scratch_shapes=[
            *[pltpu.VMEM(shape, kind) for shape, kind in scratch[:5]],
            pltpu.SemaphoreType.DMA((templates,)),
            *[pltpu.VMEM(shape, kind) for shape, kind in scratch[5:]],
        ],
        compiler_params=pltpu.CompilerParams(vmem_limit_bytes=used + 12 * 2**20),
        name="search",
    )(
        phases,
        base,
        twist,
        *pieces,
        weights,
        extra,
    )


def from_across(value, pair):
    blocks, peers = lax.axis_size("bins"), lax.axis_size("fdot")
    pairs = [
        (peers * d + f, peers * (d ^ (pair + 1 - (f ^ (f >> 1)) % 2)) + f)
        for d in range(blocks)
        for f in range(peers)
    ]
    return lax.ppermute(value, ("bins", "fdot"), pairs)


def body(spectrum, bank, fdot_index, harm_map):
    block_len = spectrum.shape[1]
    block_rows = block_len // LANES
    blocks = lax.axis_size("bins")
    templates = fdot_index.shape[0]
    part = lax.axis_index("fdot") & 1
    packed = spectrum.reshape(2, block_rows, LANES).transpose(1, 0, 2).reshape(2 * block_rows, LANES)
    mine = lax.dynamic_slice(packed, (part * block_rows, jnp.int32(0)), (block_rows, LANES))
    far = [from_across(mine, pair) for pair in range(2, blocks, 2)]
    fdot_index, phases = lax.optimization_barrier((fdot_index, harm_map[:, 0, 3]))
    weights, extra, base, twist, phases = template_rows(bank, fdot_index, phases, block_rows * blocks)
    sent, base = lax.optimization_barrier((mine, base))
    held = [sent, from_partner(sent, "bins", 1)]
    layout = [(0, 0), (1, 0)]
    for value, pair in zip(far, range(2, blocks, 2)):
        value = lax.optimization_barrier((value, base))[0]
        held += [value, from_partner(value, "fdot", 2)]
        layout += [(pair, 1), (pair, 0)]
    passed = [from_partner(value, "fdot", 1) for value in held]
    out = search(held + passed, layout, weights, extra, base, twist, phases, blocks, templates)
    return out.transpose(1, 0, 2).reshape(templates, block_len)


def solution(mesh):
    placed = (P(None, ("groups", "bins")), P(), P("fdot"), P(None, "bins", None))
    return jax.shard_map(
        body, mesh=mesh, in_specs=placed, out_specs=P("fdot", ("groups", "bins")), check_vma=False
    )
```
